128 devices in a mesh: spec: 4 (over x_lo, core), tile: 32 (over z, y, x_hi).
Axes of the slice: x: 4 (x_hi: 2, x_lo: 2; x = x_hi * 2 + x_lo), y: 4, z: 4, core: 2. Of those that a mesh axis runs over, the one named last changes fastest.
Arguments:
- tracers: float32 [288, 8, 512, 128], P('spec', None, 'tile'), may hold values from -6 to 6
- courant: float32 [4, 512, 128], P(None, 'tile'), may hold values from 0.02 to 0.22
- neighbours: int32 [2, 512, 128], P(None, 'tile'), may hold values from 0 to 127, as said below
- owner_map: int32 [32, 128], P('tile'), may hold values from 0 to 127, each once within a row
- gain: float32 [288], replicated, may hold values from 0.25 to 1.75
- w_in: bfloat16 [288, 1024], replicated, may hold values from -0.375 to 0.375
- b_in: float32 [1024], replicated, may hold values from -3 to 3
- w_mid: bfloat16 [1024, 1024], replicated, may hold values from -0.1875 to 0.1875
- b_mid: float32 [1024], replicated, may hold values from -3 to 3
- w_out: bfloat16 [1024, 288], replicated, may hold values from -0.1875 to 0.1875
Outputs:
- tracers_out: float32 [288, 8, 512, 128], P('spec', None, 'tile')
- owned_tend: bfloat16 [128, 288, 4096], P(('spec', 'tile'))
The draws below stay inside these ranges and needn't reach their ends.
Inputs may be any that keep to these rules, and one draw needn't show every extreme that they name: `neighbours`: for each cell, the y-index of its neighbour in the column before (first entry) and after (second), at most 3 rows away with wrap-around over 128. `owner_map`: each row names every owner once.
All inputs are finite; a program needn't handle non-finite values.
Results may differ from the reference program's by a relative error of at most 0.0065.
Values may be sent and summed in bfloat16 or wider, within the bound.
No kernel may reach another device: no remote copies, remote signals or barrier semaphores. Data moves between devices by JAX's collectives and lax.ppermute only.
A program may use at most 256 MiB of HBM per device.

```python
import jax
import jax.numpy as jnp
from jax import lax

SPECIES = 288
HIDDEN_W = 1024
LEV = 8
STEPS = 2
CY = 128
CB = 16
NX = 512
N_TILE = 32
DEVICES = 128


def draw_neighbours(key, part):
    key = jax.random.fold_in(key, 11)
    offset = jax.random.randint(key, (2, NX, CY), -3, 4).astype(jnp.int32)
    column = jnp.arange(CY, dtype=jnp.int32)[None, None, :]
    offset = jnp.where((column == 0) | (column == CY - 1), 0, offset)
    return ((column + offset) % CY).astype(jnp.int32)


def shard_levels(own_key, shape, cuts, low, top_value):
    level, own = 1.0, jax.random.fold_in(own_key, 6)
    for dim, parts in cuts:
        steps = jnp.exp(jax.random.uniform(jax.random.fold_in(own, dim), (parts,), jnp.float32, low / len(cuts), top_value / len(cuts)))
        level = level * jnp.repeat(steps, shape[dim] // parts).reshape([-1 if axis == dim else 1 for axis in range(len(shape))])
    return level


def bell_draw(key, extent, spread, limit, cuts=(), kind=jnp.bfloat16):
    values = jax.random.normal(key, extent, jnp.float32) * spread
    if len(cuts) > 0:
        values = shard_levels(key, extent, cuts, -0.22, 0.18) * values
    return jnp.clip(values, min=-limit, max=limit).astype(kind)


def setup_inputs(seed: int = 0) -> dict:
    splits = jax.random.split(jax.random.key(seed), 11)
    return {
        "tracers": bell_draw(splits[0], (SPECIES, LEV, NX, CY), 1.0, 6.0, ((0, 4), (2, 32)), jnp.float32),
        "courant": jnp.clip(0.02 + 0.2 * jax.random.uniform(splits[1], (4, NX, CY), jnp.float32) ** shard_levels(splits[1], (4, NX, CY), ((1, 32),), -0.2, 0.2), 0.02, 0.22),
        "neighbours": draw_neighbours(jax.random.fold_in(splits[10], 71), 0),
        "owner_map": jax.vmap(lambda own: jax.random.permutation(own, DEVICES))(jax.random.split(splits[3], N_TILE)).reshape((N_TILE, DEVICES)).astype(jnp.int32),
        "gain": jnp.clip(1.0 + 0.15 * jax.random.normal(splits[4], (SPECIES,), jnp.float32), 0.25, 1.75),
        "w_in": bell_draw(splits[5], (SPECIES, HIDDEN_W), SPECIES ** -0.5, 0.375),
        "b_in": bell_draw(splits[6], (HIDDEN_W,), 0.5, 3.0, (), jnp.float32),
        "w_mid": bell_draw(splits[7], (HIDDEN_W, HIDDEN_W), HIDDEN_W ** -0.5, 0.1875),
        "b_mid": bell_draw(splits[8], (HIDDEN_W,), 0.5, 3.0, (), jnp.float32),
        "w_out": bell_draw(splits[9], (HIDDEN_W, SPECIES), HIDDEN_W ** -0.5, 0.1875),
    }


def advect(tracer_field, courant, west_index, east_index):
    padded = jnp.pad(tracer_field, ((0, 0), (0, 0), (1, 1), (0, 0)))
    west_side = jnp.take_along_axis(padded[:, :, :-2, :], west_index, axis=3)
    east_side = jnp.take_along_axis(padded[:, :, 2:, :], east_index, axis=3)
    north_side = jnp.roll(tracer_field, -1, axis=3)
    south_side = jnp.roll(tracer_field, 1, axis=3)
    return tracer_field + courant[0] * (west_side - tracer_field) + courant[1] * (east_side - tracer_field) + courant[2] * (north_side - tracer_field) + courant[3] * (south_side - tracer_field)

def surrogate(features, gain, w_in, b_in, w_mid, b_mid, w_out):
    values = features.astype(jnp.float32)
    inv_rms = lax.rsqrt(lax.optimization_barrier(jnp.mean(values * values, axis=0, keepdims=True)) + 1e-06)
    normed = (values * inv_rms * gain[:, None]).astype(jnp.bfloat16)
    contract = (((0,), (0,)), ((), ()))
    first_sum = lax.dot_general(w_in, normed, contract, preferred_element_type=jnp.float32)
    hidden_one = jax.nn.silu(first_sum + b_in[:, None]).astype(jnp.bfloat16)
    second = lax.dot_general(w_mid, hidden_one, contract, preferred_element_type=jnp.float32)
    hidden_two = jax.nn.silu(second + b_mid[:, None]).astype(jnp.bfloat16)
    return lax.dot_general(w_out, hidden_two, contract, preferred_element_type=jnp.float32).astype(jnp.bfloat16)

def reference(tracers, courant, neighbours, owner_map, gain, w_in, b_in, w_mid, b_mid, w_out):
    west_index = jnp.broadcast_to(neighbours[0], tracers.shape)
    east_index = jnp.broadcast_to(neighbours[1], tracers.shape)
    advected = tracers
    for substep in range(STEPS):
        advected = advect(advected, courant, west_index, east_index)
    per_tile = advected.reshape(SPECIES, LEV, N_TILE, DEVICES, CB).transpose(2, 0, 1, 3, 4)

    def one_tile(tile_args):
        tile_block, owners = tile_args
        chem_in = tile_block.astype(jnp.bfloat16).reshape(SPECIES, LEV * DEVICES * CB)
        tendency = surrogate(chem_in, gain, w_in, b_in, w_mid, b_mid, w_out).reshape(SPECIES, LEV, DEVICES, CB)
        inverse = jnp.zeros((DEVICES,), jnp.int32).at[owners].set(jnp.arange(DEVICES, dtype=jnp.int32))
        owned_rows = jnp.take(tendency, inverse, axis=2).transpose(2, 0, 1, 3).reshape(DEVICES, SPECIES, LEV * CB)
        return (tile_block + tendency.astype(jnp.float32), owned_rows)
    new_tiles, owned_rows = lax.map(one_tile, (per_tile, owner_map))
    tracers_out = new_tiles.transpose(1, 2, 0, 3, 4).reshape(SPECIES, LEV, NX, CY)
    owned_tend = owned_rows.transpose(1, 2, 0, 3).reshape(DEVICES, SPECIES, N_TILE * LEV * CB)
    return (tracers_out, owned_tend)
```

```python
import functools

import jax
import jax.numpy as jnp
from jax import lax
from jax.experimental import pallas as pl
from jax.experimental.pallas import tpu as pltpu
from jax.sharding import PartitionSpec as P

LEV = 8
COLS = 16
CY = 128
BLOCK = 16
GROUP = 8
EXTRA = 16
MIB = 1024 * 1024
AXES = ("spec", "tile")
f32, bf16, i32 = jnp.float32, jnp.bfloat16, jnp.int32


def whole(shape):
    return pl.BlockSpec(shape, lambda *_: (0,) * len(shape))


def smem():
    return pl.BlockSpec(memory_space=pltpu.SMEM)


def pack_kernel(tr, courant, nbr, west, east, edge, extra):
    step = pl.program_id(0)
    species = 72
    for side, cols in ((0, (14, 15)), (1, (0, 1))):
        for j, x in enumerate(cols):
            for l in range(LEV):
                rows = tr[pl.ds(l * COLS + x, GROUP, stride=LEV * COLS), :]
                at = pl.multiple_of((j * LEV + l) * species + step * GROUP, GROUP)
                edge[side, pl.ds(at, GROUP), :] = rows

    @pl.when(step == pl.num_programs(0) - 1)
    def _():
        for side, x, out in ((0, 15, west), (1, 0, east)):
            n = 2 * LEV * species
            extra[...] = jnp.zeros_like(extra)
            for i in range(4):
                c = courant[i, x : x + 1, :]
                high = c.astype(bf16).astype(f32)
                extra[i : i + 1, :] = high
                extra[4 + i : 5 + i, :] = c - high
            for i in range(2):
                extra[8 + i : 9 + i, :] = nbr[i, x : x + 1, :].astype(f32)
            out[0:n, :] = edge[side].astype(bf16)
            out[n : n + EXTRA, :] = extra[...].astype(bf16)


def pack_halo(rows, courant, nbr):
    n = rows.shape[0] // (LEV * COLS)
    total = 2 * LEV * n + EXTRA
    out = jax.ShapeDtypeStruct((total, CY), bf16)
    return pl.pallas_call(
        pack_kernel,
        grid=(n // GROUP,),
        in_specs=[
            pl.BlockSpec((GROUP * LEV * COLS, CY), lambda c: (c, 0)),
            whole(courant.shape),
            whole(nbr.shape),
        ],
        out_specs=[whole((total, CY))] * 2,
        out_shape=[out, out],
        scratch_shapes=[pltpu.VMEM((2, 2 * LEV * n, CY), f32), pltpu.VMEM((EXTRA, CY), f32)],
        compiler_params=pltpu.CompilerParams(vmem_limit_bytes=32 * MIB),
        cost_estimate=pl.CostEstimate(flops=0, bytes_accessed=6 * MIB, transcendentals=0),
        name="pack_halo",
    )(rows, courant, nbr)


def lane_block():
    return lax.broadcasted_iota(i32, (GROUP, CY), 1) // BLOCK


def swap_blocks(tiles):
    place = lane_block()
    n = len(tiles)
    cur = [t if a == 0 else pltpu.roll(t, a * BLOCK, 1) for a, t in enumerate(tiles)]
    for bit in (1, 2, 4):
        mask = (place & bit) != 0
        cur = [jnp.where(mask, cur[(i + bit) % n], cur[i]) for i in range(n)]
    out = []
    for k in range(n):
        v = cur[(-k) % n]
        out.append(v if k == 0 else pltpu.roll(v, CY - k * BLOCK, 1))
    return out


def transport_kernel(place, tr, courant, nbr, west, east, adv, m0, m1, m2, m3, halo, coef, index, field, mid, msg):
    step = pl.program_id(0)
    species = 72
    n = 2 * LEV * species

    @pl.when(step == 0)
    def _():
        for side, src in ((0, west), (1, east)):
            halo[side] = src[...].astype(f32)
        for x in range(-1, COLS + 1):
            if x < 0 or x == COLS:
                side = 0 if x < 0 else 1
                c = [halo[side, n + i : n + i + 1, :] + halo[side, n + 4 + i : n + 5 + i, :] for i in range(4)]
                ind = [halo[side, n + 8 + i : n + 9 + i, :].astype(i32) for i in range(2)]
            else:
                c = [courant[i, x : x + 1, :] for i in range(4)]
                ind = [nbr[i, x : x + 1, :] for i in range(2)]
            c = c + [1.0 - (c[0] + c[1] + c[2] + c[3])]
            for i in range(5):
                coef[x + 1, i] = jnp.broadcast_to(c[i], (GROUP, CY))
            for i in range(2):
                index[x + 1, i] = jnp.broadcast_to(ind[i], (GROUP, CY))

    for l in range(LEV):
        for j in range(2):
            at = pl.multiple_of((j * LEV + l) * species + step * GROUP, GROUP)
            field[j, l] = halo[0, pl.ds(at, GROUP), :]
            field[COLS + 2 + j, l] = halo[1, pl.ds(at, GROUP), :]
        for x in range(COLS):
            field[x + 2, l] = tr[pl.ds(l * COLS + x, GROUP, stride=LEV * COLS), :]

    def move(src, at, l, c, ind):
        here = src[at, l]
        w = jnp.take_along_axis(src[at - 1, l], ind[0], axis=1, mode="promise_in_bounds")
        e = jnp.take_along_axis(src[at + 1, l], ind[1], axis=1, mode="promise_in_bounds")
        up = pltpu.roll(here, CY - 1, 1)
        down = pltpu.roll(here, 1, 1)
        return c[0] * w + c[1] * e + c[2] * up + c[3] * down + c[4] * here

    def first(x, _):
        c = [coef[x, i] for i in range(5)]
        ind = [index[x, i] for i in range(2)]
        for l in range(LEV):
            mid[x, l] = move(field, x + 1, l, c, ind)
        return 0

    lax.fori_loop(0, COLS + 2, first, 0)

    def second(x, _):
        c = [coef[x + 1, i] for i in range(5)]
        ind = [index[x + 1, i] for i in range(2)]
        tiles = [move(mid, x + 1, l, c, ind) for l in range(LEV)]
        for l in range(LEV):
            adv[0, x, l] = tiles[l]
        at = pl.multiple_of(step * GROUP, GROUP)
        for b, v in enumerate(swap_blocks(tiles)):
            msg[place[x * 8 + b], pl.ds(at, GROUP), :] = v
        return 0

    lax.fori_loop(0, COLS, second, 0)

    @pl.when(step == pl.num_programs(0) - 1)
    def _():
        for k, out in enumerate((m0, m1, m2, m3)):
            def put(i, _, k=k, out=out):
                pair = jnp.concatenate([msg[k * 32 + 2 * i], msg[k * 32 + 2 * i + 1]], axis=0)
                out[pl.ds(pl.multiple_of(i * 2 * species, 16), 2 * species), :] = pair.astype(bf16)
                return 0

            lax.fori_loop(0, 16, put, 0)


def transport(place, rows, courant, nbr, west, east):
    n = rows.shape[0] // (LEV * COLS)
    msg = jax.ShapeDtypeStruct((32 * n, CY), bf16)
    return pl.pallas_call(
        transport_kernel,
        grid=(n // GROUP,),
        in_specs=[
            smem(),
            pl.BlockSpec((GROUP * LEV * COLS, CY), lambda c: (c, 0)),
            whole(courant.shape),
            whole(nbr.shape),
            whole(west.shape),
            whole(east.shape),
        ],
        out_specs=[pl.BlockSpec((1, COLS, LEV, GROUP, CY), lambda c: (c, 0, 0, 0, 0))] + [whole((32 * n, CY))] * 4,
        out_shape=[jax.ShapeDtypeStruct((n // GROUP, COLS, LEV, GROUP, CY), f32)] + [msg] * 4,
        scratch_shapes=[
            pltpu.VMEM((2,) + west.shape, f32),
            pltpu.VMEM((COLS + 2, 5, GROUP, CY), f32),
            pltpu.VMEM((COLS + 2, 2, GROUP, CY), i32),
            pltpu.VMEM((COLS + 4, LEV, GROUP, CY), f32),
            pltpu.VMEM((COLS + 2, LEV, GROUP, CY), f32),
            pltpu.VMEM((128, n, CY), f32),
        ],
        compiler_params=pltpu.CompilerParams(vmem_limit_bytes=48 * MIB),
        cost_estimate=pl.CostEstimate(flops=40 * MIB, bytes_accessed=13 * MIB, transcendentals=0),
        name="transport",
    )(place, rows, courant, nbr, west, east)


def chem_kernel(slots, group, gain, w1, b1, w2, b2, w3, p0, p1, p2, p3, own, r0, r1, r2, r3, x, xn, h1, h2, y, bias, gains):
    species = 72
    total = 4 * species
    cells = slots * CY

    @pl.when(pl.program_id(0) == 0)
    def _():
        bias[0] = jnp.broadcast_to(b1[...], bias.shape[1:])
        bias[1] = jnp.broadcast_to(b2[...], bias.shape[1:])
        gains[...] = jnp.broadcast_to(gain[...], gains.shape)

    for k, piece in enumerate((p0, p1, p2, p3)):
        at = pl.multiple_of(group[k] * species, GROUP)
        for i in range(slots // 2):
            pair = piece[2 * i * species : 2 * (i + 1) * species, :].astype(f32)
            x[pl.ds(at, species), 2 * i * CY : (2 * i + 1) * CY] = pair[:species]
            x[pl.ds(at, species), (2 * i + 1) * CY : (2 * i + 2) * CY] = pair[species:]
    for i in range(slots):
        lanes = slice(i * CY, (i + 1) * CY)
        v = x[:, lanes]
        scale = lax.rsqrt(jnp.sum(v * v, axis=0, keepdims=True) * (1.0 / total) + 1e-6)
        xn[:, lanes] = (v * scale * gains[...]).astype(bf16)

    def layer(w, src, dst, b):
        hidden = w.shape[0]
        part = 256
        for m in range(0, hidden, part):
            u = jnp.dot(w[m : m + part, :], src[...], preferred_element_type=f32)
            for i in range(slots):
                lanes = slice(i * CY, (i + 1) * CY)
                v = u[:, lanes] + bias[b, m : m + part, :]
                dst[m : m + part, lanes] = (v + v * jnp.tanh(v)).astype(bf16)

    layer(w1, xn, h1, 0)
    layer(w2, h1, h2, 1)
    y[...] = jnp.dot(w3[...], h2[...], preferred_element_type=f32)
    for i in range(slots):
        own[i] = y[:, i * CY : (i + 1) * CY].astype(bf16)
    for k, piece in enumerate((r0, r1, r2, r3)):
        at = pl.multiple_of(group[k] * species, GROUP)
        for i in range(slots // 2):
            a = y[pl.ds(at, species), 2 * i * CY : (2 * i + 1) * CY]
            b = y[pl.ds(at, species), (2 * i + 1) * CY : (2 * i + 2) * CY]
            piece[2 * i * species : 2 * (i + 1) * species, :] = jnp.concatenate([a, b], axis=0).astype(bf16)


def chemistry(group, gain, w1, b1, w2, b2, w3, pieces, slots=4):
    rows = pieces[0].shape[0]
    species = 72
    total = 4 * species
    count = rows // species
    hidden = w1.shape[0]
    cells = slots * CY
    piece = pl.BlockSpec((slots * species, CY), lambda c: (c, 0))
    flops = 2 * count * CY * (hidden * hidden + 2 * hidden * total)
    return pl.pallas_call(
        functools.partial(chem_kernel, slots),
        grid=(count // slots,),
        in_specs=[smem(), whole(gain.shape), whole(w1.shape), whole(b1.shape), whole(w2.shape), whole(b2.shape), whole(w3.shape)]
        + [piece] * 4,
        out_specs=[pl.BlockSpec((slots, total, CY), lambda c: (c, 0, 0))] + [piece] * 4,
        out_shape=[jax.ShapeDtypeStruct((count, total, CY), bf16)] + [jax.ShapeDtypeStruct((rows, CY), bf16)] * 4,
        scratch_shapes=[
            pltpu.VMEM((total, cells), f32),
            pltpu.VMEM((total, cells), bf16),
            pltpu.VMEM((hidden, cells), bf16),
            pltpu.VMEM((hidden, cells), bf16),
            pltpu.VMEM((total, cells), f32),
            pltpu.VMEM((2, hidden, CY), f32),
            pltpu.VMEM((total, CY), f32),
        ],
        compiler_params=pltpu.CompilerParams(vmem_limit_bytes=48 * MIB),
        cost_estimate=pl.CostEstimate(flops=flops, bytes_accessed=11 * MIB, transcendentals=2 * hidden * count * CY),
        name="chemistry",
    )(group, gain, w1, b1, w2, b2, w3, *pieces)


def finish_kernel(place, adv, r0, r1, r2, r3, out, tend):
    step = pl.program_id(0)
    species = 72

    @pl.when(step == 0)
    def _():
        for k, piece in enumerate((r0, r1, r2, r3)):
            def take(i, _, k=k, piece=piece):
                pair = piece[pl.ds(pl.multiple_of(i * 2 * species, 16), 2 * species), :].astype(f32)
                tend[k * 32 + 2 * i] = pair[:species]
                tend[k * 32 + 2 * i + 1] = pair[species:]
                return 0

            lax.fori_loop(0, 16, take, 0)

    def column(x, _):
        at = pl.multiple_of(step * GROUP, GROUP)
        tiles = [tend[place[x * 8 + b], pl.ds(at, GROUP), :] for b in range(8)]
        for l, v in enumerate(swap_blocks(tiles)):
            out[pl.ds(l * COLS + x, GROUP, stride=LEV * COLS), :] = adv[0, x, l] + v
        return 0

    lax.fori_loop(0, COLS, column, 0)


def finish(place, adv, pieces):
    groups = adv.shape[0]
    n = groups * GROUP
    return pl.pallas_call(
        finish_kernel,
        grid=(groups,),
        in_specs=[smem(), pl.BlockSpec((1, COLS, LEV, GROUP, CY), lambda c: (c, 0, 0, 0, 0))]
        + [whole(pieces[0].shape)] * 4,
        out_specs=pl.BlockSpec((GROUP * LEV * COLS, CY), lambda c: (c, 0)),
        out_shape=jax.ShapeDtypeStruct((n * LEV * COLS, CY), f32),
        scratch_shapes=[pltpu.VMEM((128, n, CY), f32)],
        compiler_params=pltpu.CompilerParams(vmem_limit_bytes=48 * MIB),
        cost_estimate=pl.CostEstimate(flops=4 * MIB, bytes_accessed=13 * MIB, transcendentals=0),
        name="finish",
    )(place, adv, *pieces)


def sides():
    groups = []
    for core in range(2):
        for side in range(2):
            groups.append([(((t % 2) ^ side) * 2 + core) * 32 + t for t in range(32)])
    return groups


def shards(tracers, courant, neighbours, owner_map, gain, w_in, b_in, w_mid, b_mid, w_out):
    species = tracers.shape[0]
    me = lax.axis_index("spec")
    tile = lax.axis_index("tile")
    rows = tracers.reshape(-1, CY)

    west, east = pack_halo(rows, courant, neighbours)
    west = lax.ppermute(west, "tile", [(i, i + 1) for i in range(31)])
    east = lax.ppermute(east, "tile", [(i + 1, i) for i in range(31)])

    owner = owner_map[0]
    owner_spec, owner_tile = owner // 32, owner % 32
    worker = owner_spec ^ (((owner_tile ^ tile) & 1) * 2)
    place = (worker ^ me) * 32 + owner_tile
    group = jnp.arange(4, dtype=i32) ^ me

    adv, *pieces = transport(place, rows, courant, neighbours, west, east)

    def swap(parts):
        got = [lax.ppermute(parts[k], "spec", [(i, i ^ k) for i in range(4)]) for k in (2, 3, 1)]
        return [parts[0], got[2], got[0], got[1]]

    arrived = swap(pieces)
    w1 = (w_in * 0.5).T
    w2 = (w_mid * 0.5).T
    w3 = w_out.T
    own, *back = chemistry(
        group, gain[:, None], w1, 0.5 * b_in[:, None], w2, 0.5 * b_mid[:, None], w3, arrived
    )
    returned = swap(back)
    owned = lax.all_to_all(own, AXES, 0, 0, axis_index_groups=sides(), tiled=True)
    owned = owned.transpose(1, 0, 2).reshape(1, 4 * species, 32 * CY)
    out = finish(place, adv, returned)
    return out.reshape(tracers.shape), owned


def solution(mesh):
    return jax.shard_map(
        shards,
        mesh=mesh,
        in_specs=(
            P("spec", None, "tile", None),
            P(None, "tile", None),
            P(None, "tile", None),
            P("tile", None),
            P(),
            P(),
            P(),
            P(),
            P(),
            P(),
        ),
        out_specs=(P("spec", None, "tile", None), P(AXES, None, None)),
        check_vma=False,
    )
```

```python
import functools

import jax
import jax.numpy as jnp
from jax import lax
from jax.experimental import pallas as pl
from jax.experimental.pallas import tpu as pltpu
from jax.sharding import PartitionSpec as P

LEV = 8
COLS = 16
CY = 128
BLOCK = 16
GROUP = 8
EXTRA = 16
CHUNKS = (12, 12, 8)
HOME = ((0,), (1, 2))
MIB = 1024 * 1024
AXES = ("spec", "tile")
f32, bf16, i32 = jnp.float32, jnp.bfloat16, jnp.int32


def whole(shape):
    return pl.BlockSpec(shape, lambda *_: (0,) * len(shape))


def smem():
    return pl.BlockSpec(memory_space=pltpu.SMEM)


def anywhere():
    return pl.BlockSpec(memory_space=pl.ANY)


def resident():
    return pl.BlockSpec(memory_space=pltpu.VMEM)


def hbm(a):
    return pltpu.with_memory_space_constraint(a, pltpu.HBM)


def fetch_rows(rows, buf, sems, groups):
    per = GROUP * LEV * COLS
    copies = [
        pltpu.make_async_copy(rows.at[pl.ds(c * per, per), :], buf.at[pl.ds(c * per, per), :], sems.at[c])
        for c in range(groups)
    ]
    for copy in copies:
        copy.start()
    return copies


def pack_kernel(rows, courant, nbr, west, east, buf, cour, near, edge, extra, sems):
    species = 72
    groups = species // GROUP
    copies = fetch_rows(rows, buf, sems, groups)
    small = [
        pltpu.make_async_copy(courant, cour, sems.at[groups]),
        pltpu.make_async_copy(nbr, near, sems.at[groups + 1]),
    ]
    for copy in small:
        copy.start()
    for c in range(groups):
        copies[c].wait()
        for side, cols in ((0, (14, 15)), (1, (0, 1))):
            for j, x in enumerate(cols):
                for l in range(LEV):
                    at = (j * LEV + l) * species + c * GROUP
                    start = c * GROUP * LEV * COLS + l * COLS + x
                    edge[side, at : at + GROUP, :] = buf[pl.ds(start, GROUP, stride=LEV * COLS), :]
    for copy in small:
        copy.wait()
    n = 2 * LEV * species
    for side, x, out in ((0, 15, west), (1, 0, east)):
        extra[...] = jnp.zeros_like(extra)
        for i in range(4):
            v = cour[i, x : x + 1, :]
            high = v.astype(bf16).astype(f32)
            extra[i : i + 1, :] = high
            extra[4 + i : 5 + i, :] = v - high
        for i in range(2):
            extra[8 + i : 9 + i, :] = near[i, x : x + 1, :].astype(f32)
        out[0:n, :] = edge[side].astype(bf16)
        out[n : n + EXTRA, :] = extra[...].astype(bf16)


def pack_halo(rows, courant, nbr):
    n = rows.shape[0] // (LEV * COLS)
    total = 2 * LEV * n + EXTRA
    return pl.pallas_call(
        pack_kernel,
        grid=(1,),
        in_specs=[anywhere()] * 3,
        out_specs=[whole((total, CY))] * 2,
        out_shape=[pltpu.HBM((total, CY), bf16)] * 2,
        scratch_shapes=[
            pltpu.VMEM(rows.shape, f32),
            pltpu.VMEM(courant.shape, f32),
            pltpu.VMEM(nbr.shape, i32),
            pltpu.VMEM((2, 2 * LEV * n, CY), f32),
            pltpu.VMEM((EXTRA, CY), f32),
            pltpu.SemaphoreType.DMA((n // GROUP + 2,)),
        ],
        compiler_params=pltpu.CompilerParams(vmem_limit_bytes=32 * MIB),
        cost_estimate=pl.CostEstimate(flops=0, bytes_accessed=6 * MIB, transcendentals=0),
        name="pack_halo",
    )(hbm(rows), hbm(courant), hbm(nbr))


def lane_block():
    return lax.broadcasted_iota(i32, (GROUP, CY), 1) // BLOCK


def swap_blocks(tiles):
    place = lane_block()
    n = len(tiles)
    cur = [t if a == 0 else pltpu.roll(t, a * BLOCK, 1) for a, t in enumerate(tiles)]
    for bit in (1, 2, 4):
        mask = (place & bit) != 0
        cur = [jnp.where(mask, cur[(i + bit) % n], cur[i]) for i in range(n)]
    out = []
    for k in range(n):
        v = cur[(-k) % n]
        out.append(v if k == 0 else pltpu.roll(v, CY - k * BLOCK, 1))
    return out


def weights(c, ind):
    source = lax.broadcasted_iota(i32, (CY, CY), 0)
    target = lax.broadcasted_iota(i32, (CY, CY), 1)
    zero = jnp.zeros((CY, CY), f32)
    north = source == (target + 1) % CY
    south = source == (target + CY - 1) % CY
    before, after = source == ind[0], source == ind[1]
    high = [v.astype(bf16).astype(f32) for v in c]
    low = [v - h for v, h in zip(c, high)]
    stacks = []
    for pick in (
        lambda p: jnp.where(before, p[0], zero),
        lambda p: jnp.where(north, p[2], zero) + jnp.where(south, p[3], zero),
        lambda p: jnp.where(after, p[1], zero),
    ):
        h, l = pick(high).astype(bf16), pick(low).astype(bf16)
        stacks.append(jnp.concatenate([jnp.concatenate([h, l], axis=1), jnp.concatenate([h, zero.astype(bf16)], axis=1)], axis=0))
    return stacks


def split(v):
    high = v.astype(bf16)
    return jnp.concatenate([high, (v - high.astype(f32)).astype(bf16)], axis=1)


def move(cells, centre, stacks, c):
    lhs = jnp.concatenate(cells, axis=1)
    rhs = jnp.concatenate([m[: v.shape[1]] for m, v in zip(stacks, cells)], axis=0)
    both = jnp.dot(lhs, rhs, preferred_element_type=f32)
    own = 1.0 - (c[0] + c[1] + c[2] + c[3])
    return centre * own + (both[:, :CY] + both[:, CY:])


def column_weights(courant, nbr, x):
    return [courant[i, x : x + 1, :] for i in range(4)], [nbr[i, x : x + 1, :] for i in range(2)]


def put_blocks(place, msg, x, field, species):
    for c in range(species // GROUP):
        tiles = [field[l * species + c * GROUP : l * species + (c + 1) * GROUP, :] for l in range(LEV)]
        for b, v in enumerate(swap_blocks(tiles)):
            msg[place[x * 8 + b], c * GROUP : (c + 1) * GROUP, :] = v


def interior_kernel(place, rows, courant, nbr, adv, edge, filled, buf, cour, near, field, parts, mid, midparts, moved, msg, sems, out_sems, row_sems):
    species = 72
    per = LEV * COLS
    groups = species // GROUP
    copies = fetch_rows(rows, buf, sems, groups)
    small = [
        pltpu.make_async_copy(courant, cour, sems.at[groups]),
        pltpu.make_async_copy(nbr, near, sems.at[groups + 1]),
    ]
    for copy in small:
        copy.start()
    for c in range(groups):
        copies[c].wait()
        for l in range(LEV):
            for x in range(COLS):
                at = l * species + c * GROUP
                field[x, at : at + GROUP, :] = buf[pl.ds(c * GROUP * per + l * COLS + x, GROUP, stride=per), :]
    for copy in small:
        copy.wait()
    for x in range(COLS):
        parts[x] = split(field[x])
    for i, x in enumerate((0, 1, 14, 15)):
        edge[i] = field[x]
    matrices = {}
    leaving = []
    for x in range(1, COLS - 1):
        c, ind = column_weights(cour, near, x)
        matrices[x] = weights(c, ind)
        v = move([parts[x - 1], parts[x], parts[x + 1]], field[x], matrices[x], c)
        mid[x] = v
        midparts[x] = split(v)
        if x in (1, 2, 13, 14):
            edge[{1: 4, 2: 5, 13: 6, 14: 7}[x]] = v
        if x >= 3:
            y = x - 1
            c, _ = column_weights(cour, near, y)
            moved[y - 2] = move([midparts[y - 1], midparts[y], midparts[y + 1]], mid[y], matrices.pop(y), c)
            leaving.append(pltpu.make_async_copy(moved.at[y - 2], adv.at[y - 2], out_sems.at[y - 2]))
            leaving[-1].start()
            put_blocks(place, msg, y, moved.at[y - 2], species)
            for b in range(8):
                at = place[y * 8 + b]
                leaving.append(pltpu.make_async_copy(msg.at[at], filled.at[at], row_sems.at[(y - 2) * 8 + b]))
                leaving[-1].start()
    for copy in leaving:
        copy.wait()


def interior(place, rows, courant, nbr):
    n = rows.shape[0] // (LEV * COLS)
    size = (LEV * n, CY)
    wide = (LEV * n, 2 * CY)
    return pl.pallas_call(
        interior_kernel,
        in_specs=[smem()] + [anywhere()] * 3,
        out_specs=[anywhere(), whole((8,) + size), anywhere()],
        out_shape=[
            pltpu.HBM((12,) + size, f32),
            jax.ShapeDtypeStruct((8,) + size, f32),
            pltpu.HBM((128, n, CY), f32),
        ],
        scratch_shapes=[
            pltpu.VMEM(rows.shape, f32),
            pltpu.VMEM(courant.shape, f32),
            pltpu.VMEM(nbr.shape, i32),
            pltpu.VMEM((COLS,) + size, f32),
            pltpu.VMEM((COLS,) + wide, bf16),
            pltpu.VMEM((COLS,) + size, f32),
            pltpu.VMEM((COLS,) + wide, bf16),
            pltpu.VMEM((12,) + size, f32),
            pltpu.VMEM((128, n, CY), f32),
            pltpu.SemaphoreType.DMA((n // GROUP + 2,)),
            pltpu.SemaphoreType.DMA((12,)),
            pltpu.SemaphoreType.DMA((96,)),
        ],
        compiler_params=pltpu.CompilerParams(vmem_limit_bytes=48 * MIB),
        cost_estimate=pl.CostEstimate(flops=9 * 10**9, bytes_accessed=16 * MIB, transcendentals=0),
        name="interior",
    )(place, hbm(rows), hbm(courant), hbm(nbr))


def border_kernel(chunks, place, courant, nbr, west_in, east_in, edge, filled, adv, *rest):
    outs, (msg, cour, near_ind, west, east, moved, buf, sems, adv_sems, out_sems) = rest[:-10], rest[-10:]
    species = 72
    n = 2 * LEV * species
    size = LEV * species
    copies = [
        pltpu.make_async_copy(src, dst, sems.at[i])
        for i, (src, dst) in enumerate(
            ((courant, cour), (nbr, near_ind), (west_in, west), (east_in, east), (filled, msg))
        )
    ]
    for copy in copies:
        copy.start()
    for copy in copies[:4]:
        copy.wait()

    def halo_weights(halo):
        e = halo[n : n + EXTRA, :].astype(f32)
        c = [e[i : i + 1, :] + e[4 + i : 5 + i, :] for i in range(4)]
        ind = [e[8 + i : 9 + i, :].astype(i32) for i in range(2)]
        return c, ind

    leaving = []

    def place_column(i, v):
        moved[i] = v
        leaving.append(pltpu.make_async_copy(moved.at[i], adv.at[i], adv_sems.at[i]))
        leaving[-1].start()

    def parts(i):
        return split(edge[i])

    far, near = west[0:size, :], west[size:n, :]
    c, ind = halo_weights(west)
    a = split(move([far, near, parts(0)], near.astype(f32), weights(c, ind), c))
    c0, ind0 = column_weights(cour, near_ind, 0)
    m0 = weights(c0, ind0)
    b = move([near, parts(0), parts(1)], edge[0], m0, c0)
    place_column(0, move([a, split(b), parts(4)], b, m0, c0))
    c1, ind1 = column_weights(cour, near_ind, 1)
    place_column(1, move([split(b), parts(4), parts(5)], edge[4], weights(c1, ind1), c1))
    near, far = east[0:size, :], east[size:n, :]
    c, ind = halo_weights(east)
    a = split(move([parts(3), near, far], near.astype(f32), weights(c, ind), c))
    c0, ind0 = column_weights(cour, near_ind, 15)
    m0 = weights(c0, ind0)
    b = move([parts(2), parts(3), near], edge[3], m0, c0)
    place_column(3, move([parts(7), split(b), a], b, m0, c0))
    c1, ind1 = column_weights(cour, near_ind, 14)
    place_column(2, move([parts(6), parts(7), split(b)], edge[7], weights(c1, ind1), c1))

    copies[4].wait()
    for i, x in enumerate((0, 1, 14, 15)):
        put_blocks(place, msg, x, moved.at[i], species)
    first = 0
    for j, count in enumerate(chunks):
        for k in (2, 3, 1, 0):
            for i in range(first, first + count, 2):
                pair = jnp.concatenate([msg[k * 32 + i], msg[k * 32 + i + 1]], axis=0)
                buf[k, i * species : (i + 2) * species, :] = pair.astype(bf16)
            part = buf.at[k, pl.ds(first * species, count * species), :]
            leaving.append(pltpu.make_async_copy(part, outs[j * 4 + k], out_sems.at[j * 4 + k]))
            leaving[-1].start()
        first += count
    for copy in leaving:
        copy.wait()


def border(chunks, place, courant, nbr, west, east, edge, filled):
    n = filled.shape[1]
    size = (LEV * n, CY)
    pieces = [pltpu.HBM((count * n, CY), bf16) for count in chunks for _ in range(4)]
    return pl.pallas_call(
        functools.partial(border_kernel, chunks),
        in_specs=[smem()] + [anywhere()] * 4 + [whole(edge.shape), anywhere()],
        out_specs=[anywhere()] * (1 + len(pieces)),
        out_shape=[pltpu.HBM((4,) + size, f32)] + pieces,
        scratch_shapes=[
            pltpu.VMEM(filled.shape, f32),
            pltpu.VMEM(courant.shape, f32),
            pltpu.VMEM(nbr.shape, i32),
            pltpu.VMEM(west.shape, bf16),
            pltpu.VMEM(east.shape, bf16),
            pltpu.VMEM((4,) + size, f32),
            pltpu.VMEM((4, 32 * n, CY), bf16),
            pltpu.SemaphoreType.DMA((5,)),
            pltpu.SemaphoreType.DMA((4,)),
            pltpu.SemaphoreType.DMA((len(pieces),)),
        ],
        compiler_params=pltpu.CompilerParams(vmem_limit_bytes=40 * MIB),
        cost_estimate=pl.CostEstimate(flops=3 * 10**9, bytes_accessed=11 * MIB, transcendentals=0),
        name="border",
    )(place, hbm(courant), hbm(nbr), hbm(west), hbm(east), edge, hbm(filled))


def turn_kernel(gain, w_in, b_in, w_mid, b_mid, w_out, w1, w2, w3, b1, b2, g):
    half = jnp.asarray(0.5, bf16)
    w1[...] = (w_in[...] * half).T
    w2[...] = (w_mid[...] * half).T
    w3[...] = w_out[...].T
    b1[...] = jnp.broadcast_to(0.5 * b_in[...], (CY, b_in.shape[1])).T
    b2[...] = jnp.broadcast_to(0.5 * b_mid[...], (CY, b_mid.shape[1])).T
    g[...] = jnp.broadcast_to(gain[...], (CY, gain.shape[1])).T


def turn_weights(gain, w_in, b_in, w_mid, b_mid, w_out):
    species, hidden = w_in.shape
    args = (gain[None], w_in, b_in[None], w_mid, b_mid[None], w_out)
    return pl.pallas_call(
        turn_kernel,
        out_shape=[
            jax.ShapeDtypeStruct((hidden, species), bf16),
            jax.ShapeDtypeStruct((hidden, hidden), bf16),
            jax.ShapeDtypeStruct((species, hidden), bf16),
            jax.ShapeDtypeStruct((hidden, CY), f32),
            jax.ShapeDtypeStruct((hidden, CY), f32),
            jax.ShapeDtypeStruct((species, CY), f32),
        ],
        compiler_params=pltpu.CompilerParams(vmem_limit_bytes=32 * MIB),
        cost_estimate=pl.CostEstimate(flops=0, bytes_accessed=8 * MIB, transcendentals=0),
        name="turn_weights",
    )(*args)


def chem_kernel(slots, group, gain, w1, b1, w2, b2, w3, p0, p1, p2, p3, *rest):
    own, r0, r1, r2, r3, x, xn, h1, h2, y = rest[-10:]
    species = 72
    total = 4 * species

    for k, piece in enumerate((p0, p1, p2, p3)):
        at = pl.multiple_of(group[k] * species, GROUP)
        for i in range(slots // 2):
            pair = piece[2 * i * species : 2 * (i + 1) * species, :].astype(f32)
            x[pl.ds(at, species), 2 * i * CY : (2 * i + 1) * CY] = pair[:species]
            x[pl.ds(at, species), (2 * i + 1) * CY : (2 * i + 2) * CY] = pair[species:]
    for i in range(slots):
        lanes = slice(i * CY, (i + 1) * CY)
        v = x[:, lanes]
        scale = lax.rsqrt(jnp.sum(v * v, axis=0, keepdims=True) * (1.0 / total) + 1e-6)
        xn[:, lanes] = (v * scale * gain[...]).astype(bf16)

    def layer(w, src, dst, bias):
        hidden = w.shape[0]
        part = 256
        for m in range(0, hidden, part):
            u = jnp.dot(w[m : m + part, :], src[...], preferred_element_type=f32)
            for i in range(slots):
                lanes = slice(i * CY, (i + 1) * CY)
                v = u[:, lanes] + bias[m : m + part, :]
                dst[m : m + part, lanes] = (v + v * jnp.tanh(v)).astype(bf16)

    layer(w1, xn, h1, b1)
    layer(w2, h1, h2, b2)
    y[...] = jnp.dot(w3[...], h2[...], preferred_element_type=f32)
    for i in range(slots):
        own[i] = y[:, i * CY : (i + 1) * CY].astype(bf16)
    for k, piece in enumerate((r0, r1, r2, r3)):
        at = pl.multiple_of(group[k] * species, GROUP)
        for i in range(slots // 2):
            a = y[pl.ds(at, species), 2 * i * CY : (2 * i + 1) * CY]
            b = y[pl.ds(at, species), (2 * i + 1) * CY : (2 * i + 2) * CY]
            piece[2 * i * species : 2 * (i + 1) * species, :] = jnp.concatenate([a, b], axis=0).astype(bf16)


def chemistry(first, home, group, prepared, pieces, own, back, slots=4):
    w1, w2, w3, b1, b2, gain = prepared
    species = 72
    total = 4 * species
    count = pieces[0].shape[0] // species
    hidden = w1.shape[0]
    cells = slots * CY
    start, home_count = home
    piece_in = pl.BlockSpec((slots * species, CY), lambda c: (c, 0))
    piece_out = pl.BlockSpec((slots * species, CY), lambda c: ((first - start) // slots + c, 0))
    flops = 2 * count * CY * (hidden * hidden + 2 * hidden * total)
    fixed = [gain, w1, b1, w2, b2, w3]
    aliases = {}
    if own is not None:
        aliases[11] = 0
    for i in range(len(back)):
        aliases[11 + len(aliases)] = 1 + i
    handed = ([] if own is None else [own]) + list(back)
    own, *back = pl.pallas_call(
        functools.partial(chem_kernel, slots),
        grid=(count // slots,),
        in_specs=[smem()] + [resident()] * len(fixed) + [piece_in] * 4 + [anywhere()] * len(handed),
        out_specs=[pl.BlockSpec((slots, total, CY), lambda c: (first // slots + c, 0, 0))] + [piece_out] * 4,
        out_shape=[pltpu.HBM((32, total, CY), bf16)] + [pltpu.HBM((home_count * species, CY), bf16)] * 4,
        input_output_aliases=aliases,
        scratch_shapes=[
            pltpu.VMEM((total, cells), f32),
            pltpu.VMEM((total, cells), bf16),
            pltpu.VMEM((hidden, cells), bf16),
            pltpu.VMEM((hidden, cells), bf16),
            pltpu.VMEM((total, cells), f32),
        ],
        compiler_params=pltpu.CompilerParams(vmem_limit_bytes=36 * MIB),
        cost_estimate=pl.CostEstimate(flops=flops, bytes_accessed=8 * MIB, transcendentals=2 * hidden * count * CY),
        name="chemistry",
    )(group, *fixed, *[hbm(p) for p in pieces], *[hbm(a) for a in handed])
    return own, back


def finish_kernel(wide, place, middle, border, *rest):
    pieces, (out, tend) = rest[:-2], rest[-2:]
    step = pl.program_id(0)
    species = 72

    @pl.when(step == 0)
    def _():
        first = 0
        for j in range(0, len(pieces), 4):
            count = pieces[j].shape[0] // species
            for k in range(4):
                for i in range(0, count, 2):
                    pair = pieces[j + k][i * species : (i + 2) * species, :].astype(f32)
                    tend[k * 32 + first + i] = pair[:species]
                    tend[k * 32 + first + i + 1] = pair[species:]
            first += count

    for x in range(COLS):
        src, y = (middle, x - 2) if 2 <= x < 14 else (border, x if x < 2 else x - 12)
        for c in range(wide // GROUP):
            at = pl.multiple_of(step * wide + c * GROUP, GROUP)
            tiles = [tend[place[x * 8 + b], pl.ds(at, GROUP), :] for b in range(8)]
            for l, v in enumerate(swap_blocks(tiles)):
                v = v + src[y, l, c * GROUP : (c + 1) * GROUP, :]
                out[pl.ds(c * GROUP * LEV * COLS + l * COLS + x, GROUP, stride=LEV * COLS), :] = v


def finish(place, middle, border, pieces, wide=8):
    n = middle.shape[1] // LEV
    middle, border = (a.reshape(a.shape[0], LEV, n, CY) for a in (middle, border))

    def columns(a):
        return pl.BlockSpec((a.shape[0], LEV, wide, CY), lambda c: (0, 0, c, 0))

    return pl.pallas_call(
        functools.partial(finish_kernel, wide),
        grid=(n // wide,),
        in_specs=[smem(), columns(middle), columns(border)] + [whole(p.shape) for p in pieces],
        out_specs=pl.BlockSpec((wide * LEV * COLS, CY), lambda c: (c, 0)),
        out_shape=pltpu.HBM((n * LEV * COLS, CY), f32),
        scratch_shapes=[pltpu.VMEM((128, n, CY), f32)],
        compiler_params=pltpu.CompilerParams(vmem_limit_bytes=48 * MIB),
        cost_estimate=pl.CostEstimate(flops=4 * MIB, bytes_accessed=13 * MIB, transcendentals=0),
        name="finish",
    )(place, hbm(middle), hbm(border), *[hbm(p) for p in pieces])


def deliver_kernel(got, out):
    for i in range(got.shape[0]):
        out[0, :, i * CY : (i + 1) * CY] = got[i]


def deliver(got, tiles=8):
    count, total, _ = got.shape
    return pl.pallas_call(
        deliver_kernel,
        grid=(count // tiles,),
        in_specs=[pl.BlockSpec((tiles, total, CY), lambda c: (c, 0, 0))],
        out_specs=pl.BlockSpec((1, total, tiles * CY), lambda c: (0, 0, c)),
        out_shape=pltpu.HBM((1, total, count * CY), bf16),
        compiler_params=pltpu.CompilerParams(vmem_limit_bytes=32 * MIB),
        cost_estimate=pl.CostEstimate(flops=0, bytes_accessed=5 * MIB, transcendentals=0),
        name="deliver",
    )(got)


def sides():
    groups = []
    for core in range(2):
        for side in range(2):
            groups.append([(((t % 2) ^ side) * 2 + core) * 32 + t for t in range(32)])
    return groups


def shards(tracers, courant, neighbours, owner_map, gain, w_in, b_in, w_mid, b_mid, w_out):
    species = tracers.shape[0]
    me = lax.axis_index("spec")
    tile = lax.axis_index("tile")
    rows = tracers.reshape(-1, CY)

    west, east = pack_halo(rows, courant, neighbours)
    west = lax.ppermute(west, "tile", [(i, i + 1) for i in range(31)])
    east = lax.ppermute(east, "tile", [(i + 1, i) for i in range(31)])

    owner = owner_map[0]
    owner_spec, owner_tile = owner // 32, owner % 32
    worker = owner_spec ^ (((owner_tile ^ tile) & 1) * 2)
    place = (worker ^ me) * 32 + owner_tile
    group = jnp.arange(4, dtype=i32) ^ me

    middle, edge, filled = interior(place, rows, courant, neighbours)
    border_cols, *pieces = border(CHUNKS, place, courant, neighbours, west, east, edge, filled)

    def swap(parts):
        got = [lax.ppermute(parts[k], "spec", [(i, i ^ k) for i in range(4)]) for k in (2, 3, 1)]
        return [parts[0], got[2], got[0], got[1]]

    given = lax.optimization_barrier((gain, w_in, b_in, w_mid, b_mid, w_out, border_cols))[:-1]
    prepared = turn_weights(*given)
    own, returned = None, []
    for members in HOME:
        start, home_count = sum(CHUNKS[: members[0]]), sum(CHUNKS[j] for j in members)
        back = []
        for j in members:
            arrived = swap(pieces[4 * j : 4 * j + 4])
            own, back = chemistry(sum(CHUNKS[:j]), (start, home_count), group, prepared, arrived, own, back)
        returned.append(swap(back))
    own, returned[0] = lax.optimization_barrier((own, returned[0]))
    returned = [p for part in returned for p in part]
    owned = lax.all_to_all(own, AXES, 0, 0, axis_index_groups=sides(), tiled=True)
    out = finish(place, middle, border_cols, returned)
    return out.reshape(tracers.shape), deliver(owned)


def solution(mesh):
    return jax.shard_map(
        shards,
        mesh=mesh,
        in_specs=(
            P("spec", None, "tile", None),
            P(None, "tile", None),
            P(None, "tile", None),
            P("tile", None),
            P(),
            P(),
            P(),
            P(),
            P(),
            P(),
        ),
        out_specs=(P("spec", None, "tile", None), P(AXES, None, None)),
        check_vma=False,
    )
```

```python
import functools

import jax
import jax.numpy as jnp
from jax import lax
from jax.experimental import pallas as pl
from jax.experimental.pallas import tpu as pltpu
from jax.sharding import PartitionSpec as P

LEV = 8
COLS = 16
CY = 128
BLOCK = 16
GROUP = 8
EXTRA = 16
CHUNKS = (16, 16)
HOME = ((0,), (1,))
MIB = 1024 * 1024
AXES = ("spec", "tile")
f32, bf16, i32 = jnp.float32, jnp.bfloat16, jnp.int32


def whole(shape):
    return pl.BlockSpec(shape, lambda *_: (0,) * len(shape))


def smem():
    return pl.BlockSpec(memory_space=pltpu.SMEM)


def anywhere():
    return pl.BlockSpec(memory_space=pl.ANY)


def resident():
    return pl.BlockSpec(memory_space=pltpu.VMEM)


def hbm(a):
    return pltpu.with_memory_space_constraint(a, pltpu.HBM)


def fetch_rows(rows, buf, sems, groups):
    per = GROUP * LEV * COLS
    copies = [
        pltpu.make_async_copy(rows.at[pl.ds(c * per, per), :], buf.at[pl.ds(c * per, per), :], sems.at[c])
        for c in range(groups)
    ]
    for copy in copies:
        copy.start()
    return copies


def pack_kernel(rows, courant, nbr, west, east, buf, cour, near, edge, extra, sems):
    species = 72
    groups = species // GROUP
    copies = fetch_rows(rows, buf, sems, groups)
    small = [
        pltpu.make_async_copy(courant, cour, sems.at[groups]),
        pltpu.make_async_copy(nbr, near, sems.at[groups + 1]),
    ]
    for copy in small:
        copy.start()
    for c in range(groups):
        copies[c].wait()
        for side, cols in ((0, (14, 15)), (1, (0, 1))):
            for j, x in enumerate(cols):
                for l in range(LEV):
                    at = (j * LEV + l) * species + c * GROUP
                    start = c * GROUP * LEV * COLS + l * COLS + x
                    edge[side, at : at + GROUP, :] = buf[pl.ds(start, GROUP, stride=LEV * COLS), :]
    for copy in small:
        copy.wait()
    n = 2 * LEV * species
    for side, x, out in ((0, 15, west), (1, 0, east)):
        extra[...] = jnp.zeros_like(extra)
        for i in range(4):
            v = cour[i, x : x + 1, :]
            high = v.astype(bf16).astype(f32)
            extra[i : i + 1, :] = high
            extra[4 + i : 5 + i, :] = v - high
        for i in range(2):
            extra[8 + i : 9 + i, :] = near[i, x : x + 1, :].astype(f32)
        out[0:n, :] = edge[side].astype(bf16)
        out[n : n + EXTRA, :] = extra[...].astype(bf16)


def pack_halo(rows, courant, nbr):
    n = rows.shape[0] // (LEV * COLS)
    total = 2 * LEV * n + EXTRA
    return pl.pallas_call(
        pack_kernel,
        grid=(1,),
        in_specs=[anywhere()] * 3,
        out_specs=[whole((total, CY))] * 2,
        out_shape=[pltpu.HBM((total, CY), bf16)] * 2,
        scratch_shapes=[
            pltpu.VMEM(rows.shape, f32),
            pltpu.VMEM(courant.shape, f32),
            pltpu.VMEM(nbr.shape, i32),
            pltpu.VMEM((2, 2 * LEV * n, CY), f32),
            pltpu.VMEM((EXTRA, CY), f32),
            pltpu.SemaphoreType.DMA((n // GROUP + 2,)),
        ],
        compiler_params=pltpu.CompilerParams(vmem_limit_bytes=32 * MIB),
        cost_estimate=pl.CostEstimate(flops=0, bytes_accessed=6 * MIB, transcendentals=0),
        name="pack_halo",
    )(hbm(rows), hbm(courant), hbm(nbr))


def lane_block():
    return lax.broadcasted_iota(i32, (GROUP, CY), 1) // BLOCK


def swap_blocks(tiles):
    place = lane_block()
    n = len(tiles)
    cur = [t if a == 0 else pltpu.roll(t, a * BLOCK, 1) for a, t in enumerate(tiles)]
    for bit in (1, 2, 4):
        mask = (place & bit) != 0
        cur = [jnp.where(mask, cur[(i + bit) % n], cur[i]) for i in range(n)]
    out = []
    for k in range(n):
        v = cur[(-k) % n]
        out.append(v if k == 0 else pltpu.roll(v, CY - k * BLOCK, 1))
    return out


def weights(c, ind):
    source = lax.broadcasted_iota(i32, (CY, CY), 0)
    target = lax.broadcasted_iota(i32, (CY, CY), 1)
    zero = jnp.zeros((CY, CY), f32)
    north = source == (target + 1) % CY
    south = source == (target + CY - 1) % CY
    before, after = source == ind[0], source == ind[1]
    high = [v.astype(bf16).astype(f32) for v in c]
    low = [v - h for v, h in zip(c, high)]
    stacks = []
    for pick in (
        lambda p: jnp.where(before, p[0], zero),
        lambda p: jnp.where(north, p[2], zero) + jnp.where(south, p[3], zero),
        lambda p: jnp.where(after, p[1], zero),
    ):
        h, l = pick(high).astype(bf16), pick(low).astype(bf16)
        stacks.append(jnp.concatenate([jnp.concatenate([h, l], axis=1), jnp.concatenate([h, zero.astype(bf16)], axis=1)], axis=0))
    return stacks


def split(v):
    high = v.astype(bf16)
    return jnp.concatenate([high, (v - high.astype(f32)).astype(bf16)], axis=1)


def move(cells, centre, stacks, c):
    lhs = jnp.concatenate(cells, axis=1)
    rhs = jnp.concatenate([m[: v.shape[1]] for m, v in zip(stacks, cells)], axis=0)
    both = jnp.dot(lhs, rhs, preferred_element_type=f32)
    own = 1.0 - (c[0] + c[1] + c[2] + c[3])
    return centre * own + (both[:, :CY] + both[:, CY:])


def column_weights(courant, nbr, x):
    return [courant[i, x : x + 1, :] for i in range(4)], [nbr[i, x : x + 1, :] for i in range(2)]


def put_blocks(place, msg, x, field, species):
    for c in range(species // GROUP):
        tiles = [field[l * species + c * GROUP : l * species + (c + 1) * GROUP, :] for l in range(LEV)]
        for b, v in enumerate(swap_blocks(tiles)):
            msg[place[x * 8 + b], c * GROUP : (c + 1) * GROUP, :] = v


def interior_kernel(place, rows, courant, nbr, adv, edge, filled, buf, cour, near, field, parts, mid, midparts, moved, msg, sems, out_sems, row_sems):
    species = 72
    per = LEV * COLS
    groups = species // GROUP
    copies = fetch_rows(rows, buf, sems, groups)
    small = [
        pltpu.make_async_copy(courant, cour, sems.at[groups]),
        pltpu.make_async_copy(nbr, near, sems.at[groups + 1]),
    ]
    for copy in small:
        copy.start()
    for c in range(groups):
        copies[c].wait()
        for l in range(LEV):
            for x in range(COLS):
                at = l * species + c * GROUP
                field[x, at : at + GROUP, :] = buf[pl.ds(c * GROUP * per + l * COLS + x, GROUP, stride=per), :]
    for copy in small:
        copy.wait()
    for x in range(COLS):
        parts[x] = split(field[x])
    for i, x in enumerate((0, 1, 14, 15)):
        edge[i] = field[x]
    matrices = {}
    leaving = []
    for x in range(1, COLS - 1):
        c, ind = column_weights(cour, near, x)
        matrices[x] = weights(c, ind)
        v = move([parts[x - 1], parts[x], parts[x + 1]], field[x], matrices[x], c)
        mid[x] = v
        midparts[x] = split(v)
        if x in (1, 2, 13, 14):
            edge[{1: 4, 2: 5, 13: 6, 14: 7}[x]] = v
        if x >= 3:
            y = x - 1
            c, _ = column_weights(cour, near, y)
            moved[y - 2] = move([midparts[y - 1], midparts[y], midparts[y + 1]], mid[y], matrices.pop(y), c)
            leaving.append(pltpu.make_async_copy(moved.at[y - 2], adv.at[y - 2], out_sems.at[y - 2]))
            leaving[-1].start()
            put_blocks(place, msg, y, moved.at[y - 2], species)
            for b in range(8):
                at = place[y * 8 + b]
                leaving.append(pltpu.make_async_copy(msg.at[at], filled.at[at], row_sems.at[(y - 2) * 8 + b]))
                leaving[-1].start()
    for copy in leaving:
        copy.wait()


def interior(place, rows, courant, nbr):
    n = rows.shape[0] // (LEV * COLS)
    size = (LEV * n, CY)
    wide = (LEV * n, 2 * CY)
    return pl.pallas_call(
        interior_kernel,
        in_specs=[smem()] + [anywhere()] * 3,
        out_specs=[anywhere(), whole((8,) + size), anywhere()],
        out_shape=[
            pltpu.HBM((12,) + size, f32),
            jax.ShapeDtypeStruct((8,) + size, f32),
            pltpu.HBM((128, n, CY), f32),
        ],
        scratch_shapes=[
            pltpu.VMEM(rows.shape, f32),
            pltpu.VMEM(courant.shape, f32),
            pltpu.VMEM(nbr.shape, i32),
            pltpu.VMEM((COLS,) + size, f32),
            pltpu.VMEM((COLS,) + wide, bf16),
            pltpu.VMEM((COLS,) + size, f32),
            pltpu.VMEM((COLS,) + wide, bf16),
            pltpu.VMEM((12,) + size, f32),
            pltpu.VMEM((128, n, CY), f32),
            pltpu.SemaphoreType.DMA((n // GROUP + 2,)),
            pltpu.SemaphoreType.DMA((12,)),
            pltpu.SemaphoreType.DMA((96,)),
        ],
        compiler_params=pltpu.CompilerParams(vmem_limit_bytes=48 * MIB),
        cost_estimate=pl.CostEstimate(flops=9 * 10**9, bytes_accessed=16 * MIB, transcendentals=0),
        name="interior",
    )(place, hbm(rows), hbm(courant), hbm(nbr))


def border_kernel(chunks, place, courant, nbr, west_in, east_in, edge, filled, adv, *rest):
    outs, (msg, cour, near_ind, west, east, moved, buf, sems, adv_sems, out_sems) = rest[:-10], rest[-10:]
    species = 72
    n = 2 * LEV * species
    size = LEV * species
    copies = [
        pltpu.make_async_copy(src, dst, sems.at[i])
        for i, (src, dst) in enumerate(
            ((courant, cour), (nbr, near_ind), (west_in, west), (east_in, east), (filled, msg))
        )
    ]
    for copy in copies:
        copy.start()
    copies[0].wait()
    copies[1].wait()

    def halo_weights(halo):
        e = halo[n : n + EXTRA, :].astype(f32)
        c = [e[i : i + 1, :] + e[4 + i : 5 + i, :] for i in range(4)]
        ind = [e[8 + i : 9 + i, :].astype(i32) for i in range(2)]
        return c, ind

    leaving = []

    def place_column(i, v):
        moved[i] = v
        leaving.append(pltpu.make_async_copy(moved.at[i], adv.at[i], adv_sems.at[i]))
        leaving[-1].start()

    def parts(i):
        return split(edge[i])

    inner = {}
    for x in (0, 1, 15, 14):
        c, ind = column_weights(cour, near_ind, x)
        inner[x] = weights(c, ind), c
    kept = [parts(i) for i in range(8)]
    copies[2].wait()
    far, near = west[0:size, :], west[size:n, :]
    c, ind = halo_weights(west)
    b = move([near, kept[0], kept[1]], edge[0], *inner[0])
    a = split(move([far, near, kept[0]], near.astype(f32), weights(c, ind), c))
    low = split(b)
    place_column(1, move([low, kept[4], kept[5]], edge[4], *inner[1]))
    place_column(0, move([a, low, kept[4]], b, *inner[0]))
    copies[4].wait()
    for i in range(2):
        put_blocks(place, msg, i, moved.at[i], species)
    copies[3].wait()
    near, far = east[0:size, :], east[size:n, :]
    c, ind = halo_weights(east)
    b = move([kept[2], kept[3], near], edge[3], *inner[15])
    a = split(move([kept[3], near, far], near.astype(f32), weights(c, ind), c))
    low = split(b)
    place_column(2, move([kept[6], kept[7], low], edge[7], *inner[14]))
    place_column(3, move([kept[7], low, a], b, *inner[15]))
    for i in range(2, 4):
        put_blocks(place, msg, i + 12, moved.at[i], species)
    first = 0
    for j, count in enumerate(chunks):
        for k in (2, 3, 1, 0):
            for i in range(first, first + count, 2):
                pair = jnp.concatenate([msg[k * 32 + i], msg[k * 32 + i + 1]], axis=0)
                buf[k, i * species : (i + 2) * species, :] = pair.astype(bf16)
            part = buf.at[k, pl.ds(first * species, count * species), :]
            leaving.append(pltpu.make_async_copy(part, outs[j * 4 + k], out_sems.at[j * 4 + k]))
            leaving[-1].start()
        first += count
    for copy in leaving:
        copy.wait()


def border(chunks, place, courant, nbr, west, east, edge, filled):
    n = filled.shape[1]
    size = (LEV * n, CY)
    pieces = [pltpu.HBM((count * n, CY), bf16) for count in chunks for _ in range(4)]
    return pl.pallas_call(
        functools.partial(border_kernel, chunks),
        in_specs=[smem()] + [anywhere()] * 4 + [whole(edge.shape), anywhere()],
        out_specs=[anywhere()] * (1 + len(pieces)),
        out_shape=[pltpu.HBM((4,) + size, f32)] + pieces,
        scratch_shapes=[
            pltpu.VMEM(filled.shape, f32),
            pltpu.VMEM(courant.shape, f32),
            pltpu.VMEM(nbr.shape, i32),
            pltpu.VMEM(west.shape, bf16),
            pltpu.VMEM(east.shape, bf16),
            pltpu.VMEM((4,) + size, f32),
            pltpu.VMEM((4, 32 * n, CY), bf16),
            pltpu.SemaphoreType.DMA((5,)),
            pltpu.SemaphoreType.DMA((4,)),
            pltpu.SemaphoreType.DMA((len(pieces),)),
        ],
        compiler_params=pltpu.CompilerParams(vmem_limit_bytes=40 * MIB),
        cost_estimate=pl.CostEstimate(flops=3 * 10**9, bytes_accessed=11 * MIB, transcendentals=0),
        name="border",
    )(place, hbm(courant), hbm(nbr), west, east, edge, hbm(filled))


def turn_kernel(gain, w_in, b_in, w_mid, b_mid, w_out, w1, w2, w3, b1, b2, g):
    half = jnp.asarray(0.5, bf16)
    w1[...] = (w_in[...] * half).T
    w2[...] = (w_mid[...] * half).T
    w3[...] = w_out[...].T
    b1[...] = jnp.broadcast_to(0.5 * b_in[...], (CY, b_in.shape[1])).T
    b2[...] = jnp.broadcast_to(0.5 * b_mid[...], (CY, b_mid.shape[1])).T
    g[...] = jnp.broadcast_to(gain[...], (CY, gain.shape[1])).T


def turn_weights(gain, w_in, b_in, w_mid, b_mid, w_out):
    species, hidden = w_in.shape
    args = (gain[None], w_in, b_in[None], w_mid, b_mid[None], w_out)
    return pl.pallas_call(
        turn_kernel,
        out_shape=[
            jax.ShapeDtypeStruct((hidden, species), bf16),
            jax.ShapeDtypeStruct((hidden, hidden), bf16),
            jax.ShapeDtypeStruct((species, hidden), bf16),
            jax.ShapeDtypeStruct((hidden, CY), f32),
            jax.ShapeDtypeStruct((hidden, CY), f32),
            jax.ShapeDtypeStruct((species, CY), f32),
        ],
        compiler_params=pltpu.CompilerParams(vmem_limit_bytes=32 * MIB),
        cost_estimate=pl.CostEstimate(flops=0, bytes_accessed=8 * MIB, transcendentals=0),
        name="turn_weights",
    )(*args)


def chem_kernel(slots, group, gain, w1, b1, w2, b2, w3, p0, p1, p2, p3, *rest):
    own, r0, r1, r2, r3, x, xn, h1, h2, y = rest[-10:]
    species = 72
    total = 4 * species

    for k, piece in enumerate((p0, p1, p2, p3)):
        at = pl.multiple_of(group[k] * species, GROUP)
        for i in range(slots // 2):
            pair = piece[2 * i * species : 2 * (i + 1) * species, :].astype(f32)
            x[pl.ds(at, species), 2 * i * CY : (2 * i + 1) * CY] = pair[:species]
            x[pl.ds(at, species), (2 * i + 1) * CY : (2 * i + 2) * CY] = pair[species:]
    for i in range(slots):
        lanes = slice(i * CY, (i + 1) * CY)
        v = x[:, lanes]
        scale = lax.rsqrt(jnp.sum(v * v, axis=0, keepdims=True) * (1.0 / total) + 1e-6)
        xn[:, lanes] = (v * scale * gain[...]).astype(bf16)

    def layer(w, src, dst, bias):
        hidden = w.shape[0]
        part = 256
        for m in range(0, hidden, part):
            u = jnp.dot(w[m : m + part, :], src[...], preferred_element_type=f32)
            for i in range(slots):
                lanes = slice(i * CY, (i + 1) * CY)
                v = u[:, lanes] + bias[m : m + part, :]
                dst[m : m + part, lanes] = (v + v * jnp.tanh(v)).astype(bf16)

    layer(w1, xn, h1, b1)
    layer(w2, h1, h2, b2)
    y[...] = jnp.dot(w3[...], h2[...], preferred_element_type=f32)
    for i in range(slots):
        own[i] = y[:, i * CY : (i + 1) * CY].astype(bf16)
    for k, piece in enumerate((r0, r1, r2, r3)):
        at = pl.multiple_of(group[k] * species, GROUP)
        for i in range(slots // 2):
            a = y[pl.ds(at, species), 2 * i * CY : (2 * i + 1) * CY]
            b = y[pl.ds(at, species), (2 * i + 1) * CY : (2 * i + 2) * CY]
            piece[2 * i * species : 2 * (i + 1) * species, :] = jnp.concatenate([a, b], axis=0).astype(bf16)


def chemistry(first, home, group, prepared, pieces, own, back, slots=4):
    w1, w2, w3, b1, b2, gain = prepared
    species = 72
    total = 4 * species
    count = pieces[0].shape[0] // species
    hidden = w1.shape[0]
    cells = slots * CY
    start, home_count = home
    piece_in = pl.BlockSpec((slots * species, CY), lambda c: (c, 0))
    piece_out = pl.BlockSpec((slots * species, CY), lambda c: ((first - start) // slots + c, 0))
    flops = 2 * count * CY * (hidden * hidden + 2 * hidden * total)
    fixed = [gain, w1, b1, w2, b2, w3]
    aliases = {}
    if own is not None:
        aliases[11] = 0
    for i in range(len(back)):
        aliases[11 + len(aliases)] = 1 + i
    handed = ([] if own is None else [own]) + list(back)
    own, *back = pl.pallas_call(
        functools.partial(chem_kernel, slots),
        grid=(count // slots,),
        in_specs=[smem()] + [resident()] * len(fixed) + [piece_in] * 4 + [anywhere()] * len(handed),
        out_specs=[pl.BlockSpec((slots, total, CY), lambda c: (first // slots + c, 0, 0))] + [piece_out] * 4,
        out_shape=[pltpu.HBM((32, total, CY), bf16)] + [pltpu.HBM((home_count * species, CY), bf16)] * 4,
        input_output_aliases=aliases,
        scratch_shapes=[
            pltpu.VMEM((total, cells), f32),
            pltpu.VMEM((total, cells), bf16),
            pltpu.VMEM((hidden, cells), bf16),
            pltpu.VMEM((hidden, cells), bf16),
            pltpu.VMEM((total, cells), f32),
        ],
        compiler_params=pltpu.CompilerParams(vmem_limit_bytes=36 * MIB),
        cost_estimate=pl.CostEstimate(flops=flops, bytes_accessed=8 * MIB, transcendentals=2 * hidden * count * CY),
        name="chemistry",
    )(group, *fixed, *pieces, *[hbm(a) for a in handed])
    return own, back


def finish_kernel(wide, place, middle, border, *rest):
    pieces, (out, tend, cells, turn, turned) = rest[:-5], rest[-5:]
    step = pl.program_id(0)
    species = 72

    @pl.when(step == 0)
    def _():
        source = lax.broadcasted_iota(i32, (CY, LEV * CY), 0)
        target = lax.broadcasted_iota(i32, (CY, LEV * CY), 1)
        for b in range(8):
            hit = target == source // BLOCK * CY + b * BLOCK + source % BLOCK
            turn[b * CY : (b + 1) * CY, :] = jnp.where(hit, 1.0, 0.0).astype(bf16)
        first = 0
        for j in range(0, len(pieces), 4):
            count = pieces[j].shape[0] // species
            for k in range(4):
                for i in range(0, count, 2):
                    pair = pieces[j + k][i * species : (i + 2) * species, :].astype(f32)
                    tend[k * 32 + first + i] = pair[:species]
                    tend[k * 32 + first + i + 1] = pair[species:]
            first += count

    at = pl.multiple_of(step * wide, GROUP)
    for x in range(0, COLS, 2):
        for b in range(8):
            pair = [tend[place[(x + i) * 8 + b], pl.ds(at, wide), :] for i in range(2)]
            cells[x * wide : (x + 2) * wide, b * CY : (b + 1) * CY] = jnp.concatenate(pair, axis=0).astype(bf16)
    turned[...] = jnp.dot(cells[...], turn[...], preferred_element_type=f32)
    for x in range(COLS):
        src, y = (middle, x - 2) if 2 <= x < 14 else (border, x if x < 2 else x - 12)
        for c in range(wide // GROUP):
            for l in range(LEV):
                v = turned[x * wide + c * GROUP : x * wide + (c + 1) * GROUP, l * CY : (l + 1) * CY]
                v = v + src[y, l, c * GROUP : (c + 1) * GROUP, :]
                out[pl.ds(c * GROUP * LEV * COLS + l * COLS + x, GROUP, stride=LEV * COLS), :] = v


def finish(place, middle, border, pieces, wide=24):
    n = middle.shape[1] // LEV
    middle, border = (a.reshape(a.shape[0], LEV, n, CY) for a in (middle, border))

    def columns(a):
        return pl.BlockSpec((a.shape[0], LEV, wide, CY), lambda c: (0, 0, c, 0))

    return pl.pallas_call(
        functools.partial(finish_kernel, wide),
        grid=(n // wide,),
        in_specs=[smem(), columns(middle), columns(border)] + [whole(p.shape) for p in pieces],
        out_specs=pl.BlockSpec((wide * LEV * COLS, CY), lambda c: (c, 0)),
        out_shape=pltpu.HBM((n * LEV * COLS, CY), f32),
        scratch_shapes=[
            pltpu.VMEM((128, n, CY), f32),
            pltpu.VMEM((COLS * wide, LEV * CY), bf16),
            pltpu.VMEM((LEV * CY, LEV * CY), bf16),
            pltpu.VMEM((COLS * wide, LEV * CY), f32),
        ],
        compiler_params=pltpu.CompilerParams(vmem_limit_bytes=48 * MIB),
        cost_estimate=pl.CostEstimate(flops=4 * MIB, bytes_accessed=13 * MIB, transcendentals=0),
        name="finish",
    )(place, hbm(middle), hbm(border), *pieces)


def deliver_kernel(got, out):
    for i in range(got.shape[0]):
        out[0, :, i * CY : (i + 1) * CY] = got[i]


def deliver(got, tiles=8):
    count, total, _ = got.shape
    return pl.pallas_call(
        deliver_kernel,
        grid=(count // tiles,),
        in_specs=[pl.BlockSpec((tiles, total, CY), lambda c: (c, 0, 0))],
        out_specs=pl.BlockSpec((1, total, tiles * CY), lambda c: (0, 0, c)),
        out_shape=pltpu.HBM((1, total, count * CY), bf16),
        compiler_params=pltpu.CompilerParams(vmem_limit_bytes=32 * MIB),
        cost_estimate=pl.CostEstimate(flops=0, bytes_accessed=5 * MIB, transcendentals=0),
        name="deliver",
    )(got)


def sides():
    groups = []
    for core in range(2):
        for side in range(2):
            groups.append([(((t % 2) ^ side) * 2 + core) * 32 + t for t in range(32)])
    return groups


def shards(tracers, courant, neighbours, owner_map, gain, w_in, b_in, w_mid, b_mid, w_out):
    species = tracers.shape[0]
    me = lax.axis_index("spec")
    tile = lax.axis_index("tile")
    rows = tracers.reshape(-1, CY)

    west, east = pack_halo(rows, courant, neighbours)
    west = lax.ppermute(west, "tile", [(i, i + 1) for i in range(31)])
    east = lax.ppermute(east, "tile", [(i + 1, i) for i in range(31)])

    owner = owner_map[0]
    owner_spec, owner_tile = owner // 32, owner % 32
    worker = owner_spec ^ (((owner_tile ^ tile) & 1) * 2)
    place = (worker ^ me) * 32 + owner_tile
    group = jnp.arange(4, dtype=i32) ^ me

    middle, edge, filled = interior(place, rows, courant, neighbours)
    border_cols, *pieces = border(CHUNKS, place, courant, neighbours, west, east, edge, filled)

    def swap(parts):
        got = [lax.ppermute(parts[k], "spec", [(i, i ^ k) for i in range(4)]) for k in (2, 3, 1)]
        return [parts[0], got[2], got[0], got[1]]

    given = lax.optimization_barrier((gain, w_in, b_in, w_mid, b_mid, w_out, border_cols))[:-1]
    prepared = turn_weights(*given)
    own, returned = None, []
    for members in HOME:
        start, home_count = sum(CHUNKS[: members[0]]), sum(CHUNKS[j] for j in members)
        back = []
        for j in members:
            arrived = swap(pieces[4 * j : 4 * j + 4])
            own, back = chemistry(sum(CHUNKS[:j]), (start, home_count), group, prepared, arrived, own, back)
        returned.append(swap(back))
    own, returned[0] = lax.optimization_barrier((own, returned[0]))
    returned = [p for part in returned for p in part]
    owned = lax.all_to_all(own, AXES, 0, 0, axis_index_groups=sides(), tiled=True)
    out = finish(place, middle, border_cols, returned)
    return out.reshape(tracers.shape), deliver(owned)


def solution(mesh):
    return jax.shard_map(
        shards,
        mesh=mesh,
        in_specs=(
            P("spec", None, "tile", None),
            P(None, "tile", None),
            P(None, "tile", None),
            P("tile", None),
            P(),
            P(),
            P(),
            P(),
            P(),
            P(),
        ),
        out_specs=(P("spec", None, "tile", None), P(AXES, None, None)),
        check_vma=False,
    )
```

```python
import functools

import jax
import jax.numpy as jnp
from jax import lax
from jax.experimental import pallas as pl
from jax.experimental.pallas import tpu as pltpu
from jax.sharding import PartitionSpec as P

LEV = 8
COLS = 16
CY = 128
BLOCK = 16
GROUP = 8
EXTRA = 16
CHUNKS = (8, 8, 16)
HOME = ((0, 1), (2,))
MIB = 1024 * 1024
AXES = ("spec", "tile")
f32, bf16, i32 = jnp.float32, jnp.bfloat16, jnp.int32


def whole(shape):
    return pl.BlockSpec(shape, lambda *_: (0,) * len(shape))


def smem():
    return pl.BlockSpec(memory_space=pltpu.SMEM)


def anywhere():
    return pl.BlockSpec(memory_space=pl.ANY)


def resident():
    return pl.BlockSpec(memory_space=pltpu.VMEM)


def hbm(a):
    return pltpu.with_memory_space_constraint(a, pltpu.HBM)


def fetch_rows(rows, buf, sems, groups):
    per = GROUP * LEV * COLS
    copies = [
        pltpu.make_async_copy(rows.at[pl.ds(c * per, per), :], buf.at[pl.ds(c * per, per), :], sems.at[c])
        for c in range(groups)
    ]
    for copy in copies:
        copy.start()
    return copies


def pack_kernel(rows, courant, nbr, west, east, buf, cour, near, edge, extra, sems):
    species = 72
    groups = species // GROUP
    copies = fetch_rows(rows, buf, sems, groups)
    small = [
        pltpu.make_async_copy(courant, cour, sems.at[groups]),
        pltpu.make_async_copy(nbr, near, sems.at[groups + 1]),
    ]
    for copy in small:
        copy.start()
    for c in range(groups):
        copies[c].wait()
        for side, cols in ((0, (14, 15)), (1, (0, 1))):
            for j, x in enumerate(cols):
                for l in range(LEV):
                    at = (j * LEV + l) * species + c * GROUP
                    start = c * GROUP * LEV * COLS + l * COLS + x
                    edge[side, at : at + GROUP, :] = buf[pl.ds(start, GROUP, stride=LEV * COLS), :]
    for copy in small:
        copy.wait()
    n = 2 * LEV * species
    for side, x, out in ((0, 15, west), (1, 0, east)):
        extra[...] = jnp.zeros_like(extra)
        for i in range(4):
            v = cour[i, x : x + 1, :]
            high = v.astype(bf16).astype(f32)
            extra[i : i + 1, :] = high
            extra[4 + i : 5 + i, :] = v - high
        for i in range(2):
            extra[8 + i : 9 + i, :] = near[i, x : x + 1, :].astype(f32)
        out[0:n, :] = edge[side].astype(bf16)
        out[n : n + EXTRA, :] = extra[...].astype(bf16)


def pack_halo(rows, courant, nbr):
    n = rows.shape[0] // (LEV * COLS)
    total = 2 * LEV * n + EXTRA
    return pl.pallas_call(
        pack_kernel,
        grid=(1,),
        in_specs=[anywhere()] * 3,
        out_specs=[whole((total, CY))] * 2,
        out_shape=[pltpu.HBM((total, CY), bf16)] * 2,
        scratch_shapes=[
            pltpu.VMEM(rows.shape, f32),
            pltpu.VMEM(courant.shape, f32),
            pltpu.VMEM(nbr.shape, i32),
            pltpu.VMEM((2, 2 * LEV * n, CY), f32),
            pltpu.VMEM((EXTRA, CY), f32),
            pltpu.SemaphoreType.DMA((n // GROUP + 2,)),
        ],
        compiler_params=pltpu.CompilerParams(vmem_limit_bytes=32 * MIB),
        cost_estimate=pl.CostEstimate(flops=0, bytes_accessed=6 * MIB, transcendentals=0),
        name="pack_halo",
    )(hbm(rows), hbm(courant), hbm(nbr))


def lane_block():
    return lax.broadcasted_iota(i32, (GROUP, CY), 1) // BLOCK


def swap_blocks(tiles):
    place = lane_block()
    n = len(tiles)
    cur = [t if a == 0 else pltpu.roll(t, a * BLOCK, 1) for a, t in enumerate(tiles)]
    for bit in (1, 2, 4):
        mask = (place & bit) != 0
        cur = [jnp.where(mask, cur[(i + bit) % n], cur[i]) for i in range(n)]
    out = []
    for k in range(n):
        v = cur[(-k) % n]
        out.append(v if k == 0 else pltpu.roll(v, CY - k * BLOCK, 1))
    return out


def weights(c, ind):
    source = lax.broadcasted_iota(i32, (CY, CY), 0)
    target = lax.broadcasted_iota(i32, (CY, CY), 1)
    zero = jnp.zeros((CY, CY), f32)
    north = source == (target + 1) % CY
    south = source == (target + CY - 1) % CY
    before, after = source == ind[0], source == ind[1]
    high = [v.astype(bf16).astype(f32) for v in c]
    low = [v - h for v, h in zip(c, high)]
    stacks = []
    for pick in (
        lambda p: jnp.where(before, p[0], zero),
        lambda p: jnp.where(north, p[2], zero) + jnp.where(south, p[3], zero),
        lambda p: jnp.where(after, p[1], zero),
    ):
        h, l = pick(high).astype(bf16), pick(low).astype(bf16)
        stacks.append(jnp.concatenate([jnp.concatenate([h, l], axis=1), jnp.concatenate([h, zero.astype(bf16)], axis=1)], axis=0))
    return stacks


def split(v):
    high = v.astype(bf16)
    return jnp.concatenate([high, (v - high.astype(f32)).astype(bf16)], axis=1)


def move(cells, centre, stacks, c):
    lhs = jnp.concatenate(cells, axis=1)
    rhs = jnp.concatenate([m[: v.shape[1]] for m, v in zip(stacks, cells)], axis=0)
    both = jnp.dot(lhs, rhs, preferred_element_type=f32)
    own = 1.0 - (c[0] + c[1] + c[2] + c[3])
    return centre * own + (both[:, :CY] + both[:, CY:])


def column_weights(courant, nbr, x):
    return [courant[i, x : x + 1, :] for i in range(4)], [nbr[i, x : x + 1, :] for i in range(2)]


def put_blocks(place, msg, x, field, species):
    for c in range(species // GROUP):
        tiles = [field[l * species + c * GROUP : l * species + (c + 1) * GROUP, :] for l in range(LEV)]
        for b, v in enumerate(swap_blocks(tiles)):
            msg[place[x * 8 + b], c * GROUP : (c + 1) * GROUP, :] = v


def interior_kernel(place, rows, courant, nbr, adv, edge, filled, buf, cour, near, field, parts, mid, midparts, moved, msg, sems, out_sems, row_sems):
    species = 72
    per = LEV * COLS
    groups = species // GROUP
    copies = fetch_rows(rows, buf, sems, groups)
    small = [
        pltpu.make_async_copy(courant, cour, sems.at[groups]),
        pltpu.make_async_copy(nbr, near, sems.at[groups + 1]),
    ]
    for copy in small:
        copy.start()
    for c in range(groups):
        copies[c].wait()
        for l in range(LEV):
            for x in range(COLS):
                at = l * species + c * GROUP
                field[x, at : at + GROUP, :] = buf[pl.ds(c * GROUP * per + l * COLS + x, GROUP, stride=per), :]
    for copy in small:
        copy.wait()
    for x in range(COLS):
        parts[x] = split(field[x])
    for i, x in enumerate((0, 1, 14, 15)):
        edge[i] = field[x]
    matrices = {}
    leaving = []
    for x in range(1, COLS - 1):
        c, ind = column_weights(cour, near, x)
        matrices[x] = weights(c, ind)
        v = move([parts[x - 1], parts[x], parts[x + 1]], field[x], matrices[x], c)
        mid[x] = v
        midparts[x] = split(v)
        if x in (1, 2, 13, 14):
            edge[{1: 4, 2: 5, 13: 6, 14: 7}[x]] = v
        if x >= 3:
            y = x - 1
            c, _ = column_weights(cour, near, y)
            moved[y - 2] = move([midparts[y - 1], midparts[y], midparts[y + 1]], mid[y], matrices.pop(y), c)
            leaving.append(pltpu.make_async_copy(moved.at[y - 2], adv.at[y - 2], out_sems.at[y - 2]))
            leaving[-1].start()
            put_blocks(place, msg, y, moved.at[y - 2], species)
            for b in range(8):
                at = place[y * 8 + b]
                leaving.append(pltpu.make_async_copy(msg.at[at], filled.at[at], row_sems.at[(y - 2) * 8 + b]))
                leaving[-1].start()
    for copy in leaving:
        copy.wait()


def interior(place, rows, courant, nbr):
    n = rows.shape[0] // (LEV * COLS)
    size = (LEV * n, CY)
    wide = (LEV * n, 2 * CY)
    return pl.pallas_call(
        interior_kernel,
        in_specs=[smem()] + [anywhere()] * 3,
        out_specs=[anywhere(), whole((8,) + size), anywhere()],
        out_shape=[
            pltpu.HBM((12,) + size, f32),
            jax.ShapeDtypeStruct((8,) + size, f32),
            pltpu.HBM((128, n, CY), f32),
        ],
        scratch_shapes=[
            pltpu.VMEM(rows.shape, f32),
            pltpu.VMEM(courant.shape, f32),
            pltpu.VMEM(nbr.shape, i32),
            pltpu.VMEM((COLS,) + size, f32),
            pltpu.VMEM((COLS,) + wide, bf16),
            pltpu.VMEM((COLS,) + size, f32),
            pltpu.VMEM((COLS,) + wide, bf16),
            pltpu.VMEM((12,) + size, f32),
            pltpu.VMEM((128, n, CY), f32),
            pltpu.SemaphoreType.DMA((n // GROUP + 2,)),
            pltpu.SemaphoreType.DMA((12,)),
            pltpu.SemaphoreType.DMA((96,)),
        ],
        compiler_params=pltpu.CompilerParams(vmem_limit_bytes=48 * MIB),
        cost_estimate=pl.CostEstimate(flops=9 * 10**9, bytes_accessed=16 * MIB, transcendentals=0),
        name="interior",
    )(place, hbm(rows), hbm(courant), hbm(nbr))


def border_kernel(chunks, place, courant, nbr, west_in, east_in, edge, filled, adv, *rest):
    outs, (msg, cour, near_ind, west, east, moved, buf, sems, adv_sems, out_sems) = rest[:-10], rest[-10:]
    species = 72
    n = 2 * LEV * species
    size = LEV * species
    copies = [
        pltpu.make_async_copy(src, dst, sems.at[i])
        for i, (src, dst) in enumerate(
            ((courant, cour), (nbr, near_ind), (west_in, west), (east_in, east), (filled, msg))
        )
    ]
    for copy in copies:
        copy.start()
    copies[0].wait()
    copies[1].wait()

    def halo_weights(halo):
        e = halo[n : n + EXTRA, :].astype(f32)
        c = [e[i : i + 1, :] + e[4 + i : 5 + i, :] for i in range(4)]
        ind = [e[8 + i : 9 + i, :].astype(i32) for i in range(2)]
        return c, ind

    leaving = []

    def place_column(i, v):
        moved[i] = v
        leaving.append(pltpu.make_async_copy(moved.at[i], adv.at[i], adv_sems.at[i]))
        leaving[-1].start()

    def parts(i):
        return split(edge[i])

    inner = {}
    for x in (0, 1, 15, 14):
        c, ind = column_weights(cour, near_ind, x)
        inner[x] = weights(c, ind), c
    kept = [parts(i) for i in range(8)]
    copies[2].wait()
    far, near = west[0:size, :], west[size:n, :]
    c, ind = halo_weights(west)
    b = move([near, kept[0], kept[1]], edge[0], *inner[0])
    a = split(move([far, near, kept[0]], near.astype(f32), weights(c, ind), c))
    low = split(b)
    place_column(1, move([low, kept[4], kept[5]], edge[4], *inner[1]))
    place_column(0, move([a, low, kept[4]], b, *inner[0]))
    copies[4].wait()
    for i in range(2):
        put_blocks(place, msg, i, moved.at[i], species)
    copies[3].wait()
    near, far = east[0:size, :], east[size:n, :]
    c, ind = halo_weights(east)
    b = move([kept[2], kept[3], near], edge[3], *inner[15])
    a = split(move([kept[3], near, far], near.astype(f32), weights(c, ind), c))
    low = split(b)
    place_column(2, move([kept[6], kept[7], low], edge[7], *inner[14]))
    place_column(3, move([kept[7], low, a], b, *inner[15]))
    for i in range(2, 4):
        put_blocks(place, msg, i + 12, moved.at[i], species)
    first = 0
    for j, count in enumerate(chunks):
        for k in (2, 3, 1, 0):
            for i in range(first, first + count, 2):
                pair = jnp.concatenate([msg[k * 32 + i], msg[k * 32 + i + 1]], axis=0)
                buf[k, i * species : (i + 2) * species, :] = pair.astype(bf16)
            part = buf.at[k, pl.ds(first * species, count * species), :]
            leaving.append(pltpu.make_async_copy(part, outs[j * 4 + k], out_sems.at[j * 4 + k]))
            leaving[-1].start()
        first += count
    for copy in leaving:
        copy.wait()


def border(chunks, place, courant, nbr, west, east, edge, filled):
    n = filled.shape[1]
    size = (LEV * n, CY)
    pieces = [pltpu.HBM((count * n, CY), bf16) for count in chunks for _ in range(4)]
    return pl.pallas_call(
        functools.partial(border_kernel, chunks),
        in_specs=[smem()] + [anywhere()] * 4 + [whole(edge.shape), anywhere()],
        out_specs=[anywhere()] * (1 + len(pieces)),
        out_shape=[pltpu.HBM((4,) + size, f32)] + pieces,
        scratch_shapes=[
            pltpu.VMEM(filled.shape, f32),
            pltpu.VMEM(courant.shape, f32),
            pltpu.VMEM(nbr.shape, i32),
            pltpu.VMEM(west.shape, bf16),
            pltpu.VMEM(east.shape, bf16),
            pltpu.VMEM((4,) + size, f32),
            pltpu.VMEM((4, 32 * n, CY), bf16),
            pltpu.SemaphoreType.DMA((5,)),
            pltpu.SemaphoreType.DMA((4,)),
            pltpu.SemaphoreType.DMA((len(pieces),)),
        ],
        compiler_params=pltpu.CompilerParams(vmem_limit_bytes=40 * MIB),
        cost_estimate=pl.CostEstimate(flops=3 * 10**9, bytes_accessed=11 * MIB, transcendentals=0),
        name="border",
    )(place, hbm(courant), hbm(nbr), west, east, edge, hbm(filled))


def turn_kernel(gain, w_in, b_in, w_mid, b_mid, w_out, w1, w2, w3, b1, b2, g):
    half = jnp.asarray(0.5, bf16)
    w1[...] = (w_in[...] * half).T
    w2[...] = (w_mid[...] * half).T
    w3[...] = w_out[...].T
    b1[...] = jnp.broadcast_to(0.5 * b_in[...], (CY, b_in.shape[1])).T
    b2[...] = jnp.broadcast_to(0.5 * b_mid[...], (CY, b_mid.shape[1])).T
    g[...] = jnp.broadcast_to(gain[...], (CY, gain.shape[1])).T


def turn_weights(gain, w_in, b_in, w_mid, b_mid, w_out):
    species, hidden = w_in.shape
    args = (gain[None], w_in, b_in[None], w_mid, b_mid[None], w_out)
    return pl.pallas_call(
        turn_kernel,
        out_shape=[
            jax.ShapeDtypeStruct((hidden, species), bf16),
            jax.ShapeDtypeStruct((hidden, hidden), bf16),
            jax.ShapeDtypeStruct((species, hidden), bf16),
            jax.ShapeDtypeStruct((hidden, CY), f32),
            jax.ShapeDtypeStruct((hidden, CY), f32),
            jax.ShapeDtypeStruct((species, CY), f32),
        ],
        compiler_params=pltpu.CompilerParams(vmem_limit_bytes=32 * MIB),
        cost_estimate=pl.CostEstimate(flops=0, bytes_accessed=8 * MIB, transcendentals=0),
        name="turn_weights",
    )(*args)


def chem_kernel(slots, group, gain, w1, b1, w2, b2, w3, p0, p1, p2, p3, *rest):
    own, r0, r1, r2, r3, x, xn, h1, h2, y = rest[-10:]
    species = 72
    total = 4 * species

    for k, piece in enumerate((p0, p1, p2, p3)):
        at = pl.multiple_of(group[k] * species, GROUP)
        for i in range(slots // 2):
            pair = piece[2 * i * species : 2 * (i + 1) * species, :].astype(f32)
            x[pl.ds(at, species), 2 * i * CY : (2 * i + 1) * CY] = pair[:species]
            x[pl.ds(at, species), (2 * i + 1) * CY : (2 * i + 2) * CY] = pair[species:]
    for i in range(slots):
        lanes = slice(i * CY, (i + 1) * CY)
        v = x[:, lanes]
        scale = lax.rsqrt(jnp.sum(v * v, axis=0, keepdims=True) * (1.0 / total) + 1e-6)
        xn[:, lanes] = (v * scale * gain[...]).astype(bf16)

    def layer(w, src, dst, bias):
        hidden = w.shape[0]
        part = 256
        for m in range(0, hidden, part):
            u = jnp.dot(w[m : m + part, :], src[...], preferred_element_type=f32)
            for i in range(slots):
                lanes = slice(i * CY, (i + 1) * CY)
                v = u[:, lanes] + bias[m : m + part, :]
                dst[m : m + part, lanes] = (v + v * jnp.tanh(v)).astype(bf16)

    layer(w1, xn, h1, b1)
    layer(w2, h1, h2, b2)
    y[...] = jnp.dot(w3[...], h2[...], preferred_element_type=f32)
    for i in range(slots):
        own[i] = y[:, i * CY : (i + 1) * CY].astype(bf16)
    for k, piece in enumerate((r0, r1, r2, r3)):
        at = pl.multiple_of(group[k] * species, GROUP)
        for i in range(slots // 2):
            a = y[pl.ds(at, species), 2 * i * CY : (2 * i + 1) * CY]
            b = y[pl.ds(at, species), (2 * i + 1) * CY : (2 * i + 2) * CY]
            piece[2 * i * species : 2 * (i + 1) * species, :] = jnp.concatenate([a, b], axis=0).astype(bf16)


def chemistry(first, home, group, prepared, pieces, own, back, slots=4):
    w1, w2, w3, b1, b2, gain = prepared
    species = 72
    total = 4 * species
    count = pieces[0].shape[0] // species
    hidden = w1.shape[0]
    cells = slots * CY
    start, home_count = home
    piece_in = pl.BlockSpec((slots * species, CY), lambda c: (c, 0))
    piece_out = pl.BlockSpec((slots * species, CY), lambda c: ((first - start) // slots + c, 0))
    flops = 2 * count * CY * (hidden * hidden + 2 * hidden * total)
    fixed = [gain, w1, b1, w2, b2, w3]
    aliases = {}
    if own is not None:
        aliases[11] = 0
    for i in range(len(back)):
        aliases[11 + len(aliases)] = 1 + i
    handed = ([] if own is None else [own]) + list(back)
    own, *back = pl.pallas_call(
        functools.partial(chem_kernel, slots),
        grid=(count // slots,),
        in_specs=[smem()] + [resident()] * len(fixed) + [piece_in] * 4 + [anywhere()] * len(handed),
        out_specs=[pl.BlockSpec((slots, total, CY), lambda c: (first // slots + c, 0, 0))] + [piece_out] * 4,
        out_shape=[pltpu.HBM((32, total, CY), bf16)] + [pltpu.HBM((home_count * species, CY), bf16)] * 4,
        input_output_aliases=aliases,
        scratch_shapes=[
            pltpu.VMEM((total, cells), f32),
            pltpu.VMEM((total, cells), bf16),
            pltpu.VMEM((hidden, cells), bf16),
            pltpu.VMEM((hidden, cells), bf16),
            pltpu.VMEM((total, cells), f32),
        ],
        compiler_params=pltpu.CompilerParams(vmem_limit_bytes=36 * MIB),
        cost_estimate=pl.CostEstimate(flops=flops, bytes_accessed=8 * MIB, transcendentals=2 * hidden * count * CY),
        name="chemistry",
    )(group, *fixed, *pieces, *[hbm(a) for a in handed])
    return own, back


def finish_kernel(wide, place, middle, border, *rest):
    pieces, (out, tend, cells, turn, turned) = rest[:-5], rest[-5:]
    step = pl.program_id(0)
    species = 72

    @pl.when(step == 0)
    def _():
        source = lax.broadcasted_iota(i32, (CY, LEV * CY), 0)
        target = lax.broadcasted_iota(i32, (CY, LEV * CY), 1)
        for b in range(8):
            hit = target == source // BLOCK * CY + b * BLOCK + source % BLOCK
            turn[b * CY : (b + 1) * CY, :] = jnp.where(hit, 1.0, 0.0).astype(bf16)
        first = 0
        for j in range(0, len(pieces), 4):
            count = pieces[j].shape[0] // species
            for k in range(4):
                for i in range(0, count, 2):
                    pair = pieces[j + k][i * species : (i + 2) * species, :].astype(f32)
                    tend[k * 32 + first + i] = pair[:species]
                    tend[k * 32 + first + i + 1] = pair[species:]
            first += count

    at = pl.multiple_of(step * wide, GROUP)
    for x in range(0, COLS, 2):
        for b in range(8):
            pair = [tend[place[(x + i) * 8 + b], pl.ds(at, wide), :] for i in range(2)]
            cells[x * wide : (x + 2) * wide, b * CY : (b + 1) * CY] = jnp.concatenate(pair, axis=0).astype(bf16)
    turned[...] = jnp.dot(cells[...], turn[...], preferred_element_type=f32)
    for x in range(COLS):
        src, y = (middle, x - 2) if 2 <= x < 14 else (border, x if x < 2 else x - 12)
        for c in range(wide // GROUP):
            for l in range(LEV):
                v = turned[x * wide + c * GROUP : x * wide + (c + 1) * GROUP, l * CY : (l + 1) * CY]
                v = v + src[y, l, c * GROUP : (c + 1) * GROUP, :]
                out[pl.ds(c * GROUP * LEV * COLS + l * COLS + x, GROUP, stride=LEV * COLS), :] = v


def finish(place, middle, border, pieces, wide=24):
    n = middle.shape[1] // LEV
    middle, border = (a.reshape(a.shape[0], LEV, n, CY) for a in (middle, border))

    def columns(a):
        return pl.BlockSpec((a.shape[0], LEV, wide, CY), lambda c: (0, 0, c, 0))

    return pl.pallas_call(
        functools.partial(finish_kernel, wide),
        grid=(n // wide,),
        in_specs=[smem(), columns(middle), columns(border)] + [whole(p.shape) for p in pieces],
        out_specs=pl.BlockSpec((wide * LEV * COLS, CY), lambda c: (c, 0)),
        out_shape=pltpu.HBM((n * LEV * COLS, CY), f32),
        scratch_shapes=[
            pltpu.VMEM((128, n, CY), f32),
            pltpu.VMEM((COLS * wide, LEV * CY), bf16),
            pltpu.VMEM((LEV * CY, LEV * CY), bf16),
            pltpu.VMEM((COLS * wide, LEV * CY), f32),
        ],
        compiler_params=pltpu.CompilerParams(vmem_limit_bytes=48 * MIB),
        cost_estimate=pl.CostEstimate(flops=4 * MIB, bytes_accessed=13 * MIB, transcendentals=0),
        name="finish",
    )(place, hbm(middle), hbm(border), *pieces)


def deliver_kernel(got, out):
    for i in range(got.shape[0]):
        out[0, :, i * CY : (i + 1) * CY] = got[i]


def deliver(got, tiles=8):
    count, total, _ = got.shape
    return pl.pallas_call(
        deliver_kernel,
        grid=(count // tiles,),
        in_specs=[pl.BlockSpec((tiles, total, CY), lambda c: (c, 0, 0))],
        out_specs=pl.BlockSpec((1, total, tiles * CY), lambda c: (0, 0, c)),
        out_shape=pltpu.HBM((1, total, count * CY), bf16),
        compiler_params=pltpu.CompilerParams(vmem_limit_bytes=32 * MIB),
        cost_estimate=pl.CostEstimate(flops=0, bytes_accessed=5 * MIB, transcendentals=0),
        name="deliver",
    )(got)


def sides():
    groups = []
    for core in range(2):
        for side in range(2):
            groups.append([(((t % 2) ^ side) * 2 + core) * 32 + t for t in range(32)])
    return groups


def shards(tracers, courant, neighbours, owner_map, gain, w_in, b_in, w_mid, b_mid, w_out):
    species = tracers.shape[0]
    me = lax.axis_index("spec")
    tile = lax.axis_index("tile")
    rows = tracers.reshape(-1, CY)

    west, east = pack_halo(rows, courant, neighbours)
    west = lax.ppermute(west, "tile", [(i, i + 1) for i in range(31)])
    east = lax.ppermute(east, "tile", [(i + 1, i) for i in range(31)])

    owner = owner_map[0]
    owner_spec, owner_tile = owner // 32, owner % 32
    worker = owner_spec ^ (((owner_tile ^ tile) & 1) * 2)
    place = (worker ^ me) * 32 + owner_tile
    group = jnp.arange(4, dtype=i32) ^ me

    middle, edge, filled = interior(place, rows, courant, neighbours)
    border_cols, *pieces = border(CHUNKS, place, courant, neighbours, west, east, edge, filled)

    def swap(parts):
        got = [lax.ppermute(parts[k], "spec", [(i, i ^ k) for i in range(4)]) for k in (2, 3, 1)]
        return [parts[0], got[2], got[0], got[1]]

    given = lax.optimization_barrier((gain, w_in, b_in, w_mid, b_mid, w_out, border_cols))[:-1]
    prepared = turn_weights(*given)
    own, returned = None, []
    for members in HOME:
        start, home_count = sum(CHUNKS[: members[0]]), sum(CHUNKS[j] for j in members)
        back = []
        for j in members:
            arrived = swap(pieces[4 * j : 4 * j + 4])
            own, back = chemistry(sum(CHUNKS[:j]), (start, home_count), group, prepared, arrived, own, back)
        returned.append(swap(back))
    own, returned[0] = lax.optimization_barrier((own, returned[0]))
    returned = [p for part in returned for p in part]
    owned = lax.all_to_all(own, AXES, 0, 0, axis_index_groups=sides(), tiled=True)
    out = finish(place, middle, border_cols, returned)
    return out.reshape(tracers.shape), deliver(owned)


def solution(mesh):
    return jax.shard_map(
        shards,
        mesh=mesh,
        in_specs=(
            P("spec", None, "tile", None),
            P(None, "tile", None),
            P(None, "tile", None),
            P("tile", None),
            P(),
            P(),
            P(),
            P(),
            P(),
            P(),
        ),
        out_specs=(P("spec", None, "tile", None), P(AXES, None, None)),
        check_vma=False,
    )
```

```python
import functools

import jax
import jax.numpy as jnp
from jax import lax
from jax.experimental import pallas as pl
from jax.experimental.pallas import tpu as pltpu
from jax.sharding import PartitionSpec as P

LEV = 8
COLS = 16
CY = 128
BLOCK = 16
GROUP = 8
EXTRA = 16
CHUNKS = (8, 8, 16)
HOME = ((0, 1), (2,))
MIB = 1024 * 1024
AXES = ("spec", "tile")
f32, bf16, i32 = jnp.float32, jnp.bfloat16, jnp.int32


def whole(shape):
    return pl.BlockSpec(shape, lambda *_: (0,) * len(shape))


def smem():
    return pl.BlockSpec(memory_space=pltpu.SMEM)


def anywhere():
    return pl.BlockSpec(memory_space=pl.ANY)


def resident():
    return pl.BlockSpec(memory_space=pltpu.VMEM)


def hbm(a):
    return pltpu.with_memory_space_constraint(a, pltpu.HBM)


def fetch_rows(rows, buf, sems, groups):
    per = GROUP * LEV * COLS
    copies = [
        pltpu.make_async_copy(rows.at[pl.ds(c * per, per), :], buf.at[pl.ds(c * per, per), :], sems.at[c])
        for c in range(groups)
    ]
    for copy in copies:
        copy.start()
    return copies


def pack_kernel(rows, courant, nbr, west, east, buf, cour, near, edge, extra, sems):
    species = 72
    groups = species // GROUP
    copies = fetch_rows(rows, buf, sems, groups)
    small = [
        pltpu.make_async_copy(courant, cour, sems.at[groups]),
        pltpu.make_async_copy(nbr, near, sems.at[groups + 1]),
    ]
    for copy in small:
        copy.start()
    for c in range(groups):
        copies[c].wait()
        for side, cols in ((0, (14, 15)), (1, (0, 1))):
            for j, x in enumerate(cols):
                for l in range(LEV):
                    at = (j * LEV + l) * species + c * GROUP
                    start = c * GROUP * LEV * COLS + l * COLS + x
                    edge[side, at : at + GROUP, :] = buf[pl.ds(start, GROUP, stride=LEV * COLS), :]
    for copy in small:
        copy.wait()
    n = 2 * LEV * species
    for side, x, out in ((0, 15, west), (1, 0, east)):
        extra[...] = jnp.zeros_like(extra)
        for i in range(4):
            v = cour[i, x : x + 1, :]
            high = v.astype(bf16).astype(f32)
            extra[i : i + 1, :] = high
            extra[4 + i : 5 + i, :] = v - high
        for i in range(2):
            extra[8 + i : 9 + i, :] = near[i, x : x + 1, :].astype(f32)
        out[0:n, :] = edge[side].astype(bf16)
        out[n : n + EXTRA, :] = extra[...].astype(bf16)


def pack_halo(rows, courant, nbr):
    n = rows.shape[0] // (LEV * COLS)
    total = 2 * LEV * n + EXTRA
    return pl.pallas_call(
        pack_kernel,
        grid=(1,),
        in_specs=[anywhere()] * 3,
        out_specs=[whole((total, CY))] * 2,
        out_shape=[pltpu.HBM((total, CY), bf16)] * 2,
        scratch_shapes=[
            pltpu.VMEM(rows.shape, f32),
            pltpu.VMEM(courant.shape, f32),
            pltpu.VMEM(nbr.shape, i32),
            pltpu.VMEM((2, 2 * LEV * n, CY), f32),
            pltpu.VMEM((EXTRA, CY), f32),
            pltpu.SemaphoreType.DMA((n // GROUP + 2,)),
        ],
        compiler_params=pltpu.CompilerParams(vmem_limit_bytes=32 * MIB),
        cost_estimate=pl.CostEstimate(flops=0, bytes_accessed=6 * MIB, transcendentals=0),
        name="pack_halo",
    )(hbm(rows), hbm(courant), hbm(nbr))


def lane_block():
    return lax.broadcasted_iota(i32, (GROUP, CY), 1) // BLOCK


def swap_blocks(tiles):
    place = lane_block()
    n = len(tiles)
    cur = [t if a == 0 else pltpu.roll(t, a * BLOCK, 1) for a, t in enumerate(tiles)]
    for bit in (1, 2, 4):
        mask = (place & bit) != 0
        cur = [jnp.where(mask, cur[(i + bit) % n], cur[i]) for i in range(n)]
    out = []
    for k in range(n):
        v = cur[(-k) % n]
        out.append(v if k == 0 else pltpu.roll(v, CY - k * BLOCK, 1))
    return out


def weights(c, ind):
    source = lax.broadcasted_iota(i32, (CY, CY), 0)
    target = lax.broadcasted_iota(i32, (CY, CY), 1)
    zero = jnp.zeros((CY, CY), f32)
    north = source == (target + 1) % CY
    south = source == (target + CY - 1) % CY
    before, after = source == ind[0], source == ind[1]
    high = [v.astype(bf16).astype(f32) for v in c]
    low = [v - h for v, h in zip(c, high)]
    stacks = []
    for pick in (
        lambda p: jnp.where(before, p[0], zero),
        lambda p: jnp.where(north, p[2], zero) + jnp.where(south, p[3], zero),
        lambda p: jnp.where(after, p[1], zero),
    ):
        h, l = pick(high).astype(bf16), pick(low).astype(bf16)
        stacks.append(jnp.concatenate([jnp.concatenate([h, l], axis=1), jnp.concatenate([h, zero.astype(bf16)], axis=1)], axis=0))
    return stacks


def split(v):
    high = v.astype(bf16)
    return jnp.concatenate([high, (v - high.astype(f32)).astype(bf16)], axis=1)


def move(cells, centre, stacks, c):
    lhs = jnp.concatenate(cells, axis=1)
    rhs = jnp.concatenate([m[: v.shape[1]] for m, v in zip(stacks, cells)], axis=0)
    both = jnp.dot(lhs, rhs, preferred_element_type=f32)
    own = 1.0 - (c[0] + c[1] + c[2] + c[3])
    return centre * own + (both[:, :CY] + both[:, CY:])


def column_weights(courant, nbr, x):
    return [courant[i, x : x + 1, :] for i in range(4)], [nbr[i, x : x + 1, :] for i in range(2)]


def put_blocks(place, msg, x, field, species):
    for c in range(species // GROUP):
        tiles = [field[l * species + c * GROUP : l * species + (c + 1) * GROUP, :] for l in range(LEV)]
        for b, v in enumerate(swap_blocks(tiles)):
            msg[place[x * 8 + b], c * GROUP : (c + 1) * GROUP, :] = v


def interior_kernel(place, rows, courant, nbr, adv, edge, filled, buf, cour, near, field, parts, mid, midparts, moved, msg, sems, out_sems, row_sems):
    species = 72
    per = LEV * COLS
    groups = species // GROUP
    copies = fetch_rows(rows, buf, sems, groups)
    small = [
        pltpu.make_async_copy(courant, cour, sems.at[groups]),
        pltpu.make_async_copy(nbr, near, sems.at[groups + 1]),
    ]
    for copy in small:
        copy.start()
    for c in range(groups):
        copies[c].wait()
        for l in range(LEV):
            for x in range(COLS):
                at = l * species + c * GROUP
                field[x, at : at + GROUP, :] = buf[pl.ds(c * GROUP * per + l * COLS + x, GROUP, stride=per), :]
    for copy in small:
        copy.wait()
    for x in range(COLS):
        parts[x] = split(field[x])
    for i, x in enumerate((0, 1, 14, 15)):
        edge[i] = field[x]
    matrices = {}
    leaving = []
    for x in range(1, COLS - 1):
        c, ind = column_weights(cour, near, x)
        matrices[x] = weights(c, ind)
        v = move([parts[x - 1], parts[x], parts[x + 1]], field[x], matrices[x], c)
        mid[x] = v
        midparts[x] = split(v)
        if x in (1, 2, 13, 14):
            edge[{1: 4, 2: 5, 13: 6, 14: 7}[x]] = v
        if x >= 3:
            y = x - 1
            c, _ = column_weights(cour, near, y)
            moved[y - 2] = move([midparts[y - 1], midparts[y], midparts[y + 1]], mid[y], matrices.pop(y), c)
            leaving.append(pltpu.make_async_copy(moved.at[y - 2], adv.at[y - 2], out_sems.at[y - 2]))
            leaving[-1].start()
            put_blocks(place, msg, y, moved.at[y - 2], species)
            for b in range(8):
                at = place[y * 8 + b]
                leaving.append(pltpu.make_async_copy(msg.at[at], filled.at[at], row_sems.at[(y - 2) * 8 + b]))
                leaving[-1].start()
    for copy in leaving:
        copy.wait()


def interior(place, rows, courant, nbr):
    n = rows.shape[0] // (LEV * COLS)
    size = (LEV * n, CY)
    wide = (LEV * n, 2 * CY)
    return pl.pallas_call(
        interior_kernel,
        in_specs=[smem()] + [anywhere()] * 3,
        out_specs=[anywhere(), whole((8,) + size), anywhere()],
        out_shape=[
            pltpu.HBM((12,) + size, f32),
            jax.ShapeDtypeStruct((8,) + size, f32),
            pltpu.HBM((128, n, CY), f32),
        ],
        scratch_shapes=[
            pltpu.VMEM(rows.shape, f32),
            pltpu.VMEM(courant.shape, f32),
            pltpu.VMEM(nbr.shape, i32),
            pltpu.VMEM((COLS,) + size, f32),
            pltpu.VMEM((COLS,) + wide, bf16),
            pltpu.VMEM((COLS,) + size, f32),
            pltpu.VMEM((COLS,) + wide, bf16),
            pltpu.VMEM((12,) + size, f32),
            pltpu.VMEM((128, n, CY), f32),
            pltpu.SemaphoreType.DMA((n // GROUP + 2,)),
            pltpu.SemaphoreType.DMA((12,)),
            pltpu.SemaphoreType.DMA((96,)),
        ],
        compiler_params=pltpu.CompilerParams(vmem_limit_bytes=48 * MIB),
        cost_estimate=pl.CostEstimate(flops=9 * 10**9, bytes_accessed=16 * MIB, transcendentals=0),
        name="interior",
    )(place, hbm(rows), hbm(courant), hbm(nbr))


def border_kernel(chunks, place, courant, nbr, west_in, east_in, edge, filled, adv, *rest):
    outs, (msg, cour, near_ind, west, east, moved, buf, sems, adv_sems, out_sems) = rest[:-10], rest[-10:]
    species = 72
    n = 2 * LEV * species
    size = LEV * species
    copies = [
        pltpu.make_async_copy(src, dst, sems.at[i])
        for i, (src, dst) in enumerate(
            ((courant, cour), (nbr, near_ind), (west_in, west), (east_in, east), (filled, msg))
        )
    ]
    for copy in copies:
        copy.start()
    copies[0].wait()
    copies[1].wait()

    def halo_weights(halo):
        e = halo[n : n + EXTRA, :].astype(f32)
        c = [e[i : i + 1, :] + e[4 + i : 5 + i, :] for i in range(4)]
        ind = [e[8 + i : 9 + i, :].astype(i32) for i in range(2)]
        return c, ind

    leaving = []

    def place_column(i, v):
        moved[i] = v
        leaving.append(pltpu.make_async_copy(moved.at[i], adv.at[i], adv_sems.at[i]))
        leaving[-1].start()

    def parts(i):
        return split(edge[i])

    inner = {}
    for x in (0, 1, 15, 14):
        c, ind = column_weights(cour, near_ind, x)
        inner[x] = weights(c, ind), c
    kept = [parts(i) for i in range(8)]
    copies[2].wait()
    far, near = west[0:size, :], west[size:n, :]
    c, ind = halo_weights(west)
    b = move([near, kept[0], kept[1]], edge[0], *inner[0])
    a = split(move([far, near, kept[0]], near.astype(f32), weights(c, ind), c))
    low = split(b)
    place_column(1, move([low, kept[4], kept[5]], edge[4], *inner[1]))
    place_column(0, move([a, low, kept[4]], b, *inner[0]))
    copies[4].wait()
    for i in range(2):
        put_blocks(place, msg, i, moved.at[i], species)
    copies[3].wait()
    near, far = east[0:size, :], east[size:n, :]
    c, ind = halo_weights(east)
    b = move([kept[2], kept[3], near], edge[3], *inner[15])
    a = split(move([kept[3], near, far], near.astype(f32), weights(c, ind), c))
    low = split(b)
    place_column(2, move([kept[6], kept[7], low], edge[7], *inner[14]))
    place_column(3, move([kept[7], low, a], b, *inner[15]))
    for i in range(2, 4):
        put_blocks(place, msg, i + 12, moved.at[i], species)
    first = 0
    for j, count in enumerate(chunks):
        for k in (2, 3, 1, 0):
            for i in range(first, first + count, 2):
                pair = jnp.concatenate([msg[k * 32 + i], msg[k * 32 + i + 1]], axis=0)
                buf[k, i * species : (i + 2) * species, :] = pair.astype(bf16)
            part = buf.at[k, pl.ds(first * species, count * species), :]
            leaving.append(pltpu.make_async_copy(part, outs[j * 4 + k], out_sems.at[j * 4 + k]))
            leaving[-1].start()
        first += count
    for copy in leaving:
        copy.wait()


def border(chunks, place, courant, nbr, west, east, edge, filled):
    n = filled.shape[1]
    size = (LEV * n, CY)
    pieces = [pltpu.HBM((count * n, CY), bf16) for count in chunks for _ in range(4)]
    return pl.pallas_call(
        functools.partial(border_kernel, chunks),
        in_specs=[smem()] + [anywhere()] * 4 + [whole(edge.shape), anywhere()],
        out_specs=[anywhere()] * (1 + len(pieces)),
        out_shape=[pltpu.HBM((4,) + size, f32)] + pieces,
        scratch_shapes=[
            pltpu.VMEM(filled.shape, f32),
            pltpu.VMEM(courant.shape, f32),
            pltpu.VMEM(nbr.shape, i32),
            pltpu.VMEM(west.shape, bf16),
            pltpu.VMEM(east.shape, bf16),
            pltpu.VMEM((4,) + size, f32),
            pltpu.VMEM((4, 32 * n, CY), bf16),
            pltpu.SemaphoreType.DMA((5,)),
            pltpu.SemaphoreType.DMA((4,)),
            pltpu.SemaphoreType.DMA((len(pieces),)),
        ],
        compiler_params=pltpu.CompilerParams(vmem_limit_bytes=40 * MIB),
        cost_estimate=pl.CostEstimate(flops=3 * 10**9, bytes_accessed=11 * MIB, transcendentals=0),
        name="border",
    )(place, hbm(courant), hbm(nbr), west, east, edge, hbm(filled))


def turn_kernel(gain, w_in, b_in, w_mid, b_mid, w_out, w1, w2, w3, b1, b2, g):
    half = jnp.asarray(0.5, bf16)
    w1[...] = (w_in[...] * half).T
    w2[...] = (w_mid[...] * half).T
    w3[...] = w_out[...].T
    b1[...] = jnp.broadcast_to(0.5 * b_in[...], (CY, b_in.shape[1])).T
    b2[...] = jnp.broadcast_to(0.5 * b_mid[...], (CY, b_mid.shape[1])).T
    g[...] = jnp.broadcast_to(gain[...], (CY, gain.shape[1])).T


def turn_weights(gain, w_in, b_in, w_mid, b_mid, w_out):
    species, hidden = w_in.shape
    args = (gain[None], w_in, b_in[None], w_mid, b_mid[None], w_out)
    return pl.pallas_call(
        turn_kernel,
        out_shape=[
            jax.ShapeDtypeStruct((hidden, species), bf16),
            jax.ShapeDtypeStruct((hidden, hidden), bf16),
            jax.ShapeDtypeStruct((species, hidden), bf16),
            jax.ShapeDtypeStruct((hidden, CY), f32),
            jax.ShapeDtypeStruct((hidden, CY), f32),
            jax.ShapeDtypeStruct((species, CY), f32),
        ],
        compiler_params=pltpu.CompilerParams(vmem_limit_bytes=32 * MIB),
        cost_estimate=pl.CostEstimate(flops=0, bytes_accessed=8 * MIB, transcendentals=0),
        name="turn_weights",
    )(*args)


def chem_kernel(slots, group, gain, w1, b1, w2, b2, w3, p0, p1, p2, p3, *rest):
    own, r0, r1, r2, r3, x, xn, h1, h2, y = rest[-10:]
    species = 72
    total = 4 * species

    for k, piece in enumerate((p0, p1, p2, p3)):
        at = pl.multiple_of(group[k] * species, GROUP)
        for i in range(slots // 2):
            pair = piece[2 * i * species : 2 * (i + 1) * species, :].astype(f32)
            x[pl.ds(at, species), 2 * i * CY : (2 * i + 1) * CY] = pair[:species]
            x[pl.ds(at, species), (2 * i + 1) * CY : (2 * i + 2) * CY] = pair[species:]
    for i in range(slots):
        lanes = slice(i * CY, (i + 1) * CY)
        v = x[:, lanes]
        scale = lax.rsqrt(jnp.sum(v * v, axis=0, keepdims=True) * (1.0 / total) + 1e-6)
        xn[:, lanes] = (v * scale * gain[...]).astype(bf16)

    def layer(w, src, dst, bias):
        hidden = w.shape[0]
        part = 256
        for m in range(0, hidden, part):
            u = jnp.dot(w[m : m + part, :], src[...], preferred_element_type=f32)
            for i in range(slots):
                lanes = slice(i * CY, (i + 1) * CY)
                v = u[:, lanes] + bias[m : m + part, :]
                dst[m : m + part, lanes] = (v + v * jnp.tanh(v)).astype(bf16)

    layer(w1, xn, h1, b1)
    layer(w2, h1, h2, b2)
    y[...] = jnp.dot(w3[...], h2[...], preferred_element_type=f32)
    for i in range(slots):
        own[i] = y[:, i * CY : (i + 1) * CY].astype(bf16)
    for k, piece in enumerate((r0, r1, r2, r3)):
        at = pl.multiple_of(group[k] * species, GROUP)
        for i in range(slots // 2):
            a = y[pl.ds(at, species), 2 * i * CY : (2 * i + 1) * CY]
            b = y[pl.ds(at, species), (2 * i + 1) * CY : (2 * i + 2) * CY]
            piece[2 * i * species : 2 * (i + 1) * species, :] = jnp.concatenate([a, b], axis=0).astype(bf16)


def chemistry(first, home, group, prepared, pieces, own, back, slots=8):
    w1, w2, w3, b1, b2, gain = prepared
    species = 72
    total = 4 * species
    count = pieces[0].shape[0] // species
    hidden = w1.shape[0]
    cells = slots * CY
    start, home_count = home
    piece_in = pl.BlockSpec((slots * species, CY), lambda c: (c, 0))
    piece_out = pl.BlockSpec((slots * species, CY), lambda c: ((first - start) // slots + c, 0))
    flops = 2 * count * CY * (hidden * hidden + 2 * hidden * total)
    fixed = [gain, w1, b1, w2, b2, w3]
    aliases = {}
    if own is not None:
        aliases[11] = 0
    for i in range(len(back)):
        aliases[11 + len(aliases)] = 1 + i
    handed = ([] if own is None else [own]) + list(back)
    own, *back = pl.pallas_call(
        functools.partial(chem_kernel, slots),
        grid=(count // slots,),
        in_specs=[smem()] + [resident()] * len(fixed) + [piece_in] * 4 + [anywhere()] * len(handed),
        out_specs=[pl.BlockSpec((slots, total, CY), lambda c: (first // slots + c, 0, 0))] + [piece_out] * 4,
        out_shape=[pltpu.HBM((32, total, CY), bf16)] + [pltpu.HBM((home_count * species, CY), bf16)] * 4,
        input_output_aliases=aliases,
        scratch_shapes=[
            pltpu.VMEM((total, cells), f32),
            pltpu.VMEM((total, cells), bf16),
            pltpu.VMEM((hidden, cells), bf16),
            pltpu.VMEM((hidden, cells), bf16),
            pltpu.VMEM((total, cells), f32),
        ],
        compiler_params=pltpu.CompilerParams(vmem_limit_bytes=36 * MIB),
        cost_estimate=pl.CostEstimate(flops=flops, bytes_accessed=8 * MIB, transcendentals=2 * hidden * count * CY),
        name="chemistry",
    )(group, *fixed, *pieces, *[hbm(a) for a in handed])
    return own, back


def finish_kernel(wide, place, middle, border, *rest):
    pieces, (out, tend, cells, turn, turned) = rest[:-5], rest[-5:]
    step = pl.program_id(0)
    species = 72

    @pl.when(step == 0)
    def _():
        source = lax.broadcasted_iota(i32, (CY, LEV * CY), 0)
        target = lax.broadcasted_iota(i32, (CY, LEV * CY), 1)
        for b in range(8):
            hit = target == source // BLOCK * CY + b * BLOCK + source % BLOCK
            turn[b * CY : (b + 1) * CY, :] = jnp.where(hit, 1.0, 0.0).astype(bf16)
        first = 0
        for j in range(0, len(pieces), 4):
            count = pieces[j].shape[0] // species
            for k in range(4):
                for i in range(0, count, 2):
                    pair = pieces[j + k][i * species : (i + 2) * species, :].astype(f32)
                    tend[k * 32 + first + i] = pair[:species]
                    tend[k * 32 + first + i + 1] = pair[species:]
            first += count

    at = pl.multiple_of(step * wide, GROUP)
    for x in range(0, COLS, 2):
        for b in range(8):
            pair = [tend[place[(x + i) * 8 + b], pl.ds(at, wide), :] for i in range(2)]
            cells[x * wide : (x + 2) * wide, b * CY : (b + 1) * CY] = jnp.concatenate(pair, axis=0).astype(bf16)
    turned[...] = jnp.dot(cells[...], turn[...], preferred_element_type=f32)
    for x in range(COLS):
        src, y = (middle, x - 2) if 2 <= x < 14 else (border, x if x < 2 else x - 12)
        for c in range(wide // GROUP):
            for l in range(LEV):
                v = turned[x * wide + c * GROUP : x * wide + (c + 1) * GROUP, l * CY : (l + 1) * CY]
                v = v + src[y, l, c * GROUP : (c + 1) * GROUP, :]
                out[pl.ds(c * GROUP * LEV * COLS + l * COLS + x, GROUP, stride=LEV * COLS), :] = v


def finish(place, middle, border, pieces, wide=24):
    n = middle.shape[1] // LEV
    middle, border = (a.reshape(a.shape[0], LEV, n, CY) for a in (middle, border))

    def columns(a):
        return pl.BlockSpec((a.shape[0], LEV, wide, CY), lambda c: (0, 0, c, 0))

    return pl.pallas_call(
        functools.partial(finish_kernel, wide),
        grid=(n // wide,),
        in_specs=[smem(), columns(middle), columns(border)] + [whole(p.shape) for p in pieces],
        out_specs=pl.BlockSpec((wide * LEV * COLS, CY), lambda c: (c, 0)),
        out_shape=pltpu.HBM((n * LEV * COLS, CY), f32),
        scratch_shapes=[
            pltpu.VMEM((128, n, CY), f32),
            pltpu.VMEM((COLS * wide, LEV * CY), bf16),
            pltpu.VMEM((LEV * CY, LEV * CY), bf16),
            pltpu.VMEM((COLS * wide, LEV * CY), f32),
        ],
        compiler_params=pltpu.CompilerParams(vmem_limit_bytes=48 * MIB),
        cost_estimate=pl.CostEstimate(flops=4 * MIB, bytes_accessed=13 * MIB, transcendentals=0),
        name="finish",
    )(place, hbm(middle), hbm(border), *pieces)


def deliver_kernel(got, out):
    for i in range(got.shape[0]):
        out[0, :, i * CY : (i + 1) * CY] = got[i]


def deliver(got, tiles=8):
    count, total, _ = got.shape
    return pl.pallas_call(
        deliver_kernel,
        grid=(count // tiles,),
        in_specs=[pl.BlockSpec((tiles, total, CY), lambda c: (c, 0, 0))],
        out_specs=pl.BlockSpec((1, total, tiles * CY), lambda c: (0, 0, c)),
        out_shape=pltpu.HBM((1, total, count * CY), bf16),
        compiler_params=pltpu.CompilerParams(vmem_limit_bytes=32 * MIB),
        cost_estimate=pl.CostEstimate(flops=0, bytes_accessed=5 * MIB, transcendentals=0),
        name="deliver",
    )(got)


def sides():
    groups = []
    for core in range(2):
        for side in range(2):
            groups.append([(((t % 2) ^ side) * 2 + core) * 32 + t for t in range(32)])
    return groups


def shards(tracers, courant, neighbours, owner_map, gain, w_in, b_in, w_mid, b_mid, w_out):
    species = tracers.shape[0]
    me = lax.axis_index("spec")
    tile = lax.axis_index("tile")
    rows = tracers.reshape(-1, CY)

    west, east = pack_halo(rows, courant, neighbours)
    west = lax.ppermute(west, "tile", [(i, i + 1) for i in range(31)])
    east = lax.ppermute(east, "tile", [(i + 1, i) for i in range(31)])

    owner = owner_map[0]
    owner_spec, owner_tile = owner // 32, owner % 32
    worker = owner_spec ^ (((owner_tile ^ tile) & 1) * 2)
    place = (worker ^ me) * 32 + owner_tile
    group = jnp.arange(4, dtype=i32) ^ me

    middle, edge, filled = interior(place, rows, courant, neighbours)
    border_cols, *pieces = border(CHUNKS, place, courant, neighbours, west, east, edge, filled)

    def swap(parts):
        got = [lax.ppermute(parts[k], "spec", [(i, i ^ k) for i in range(4)]) for k in (2, 3, 1)]
        return [parts[0], got[2], got[0], got[1]]

    given = lax.optimization_barrier((gain, w_in, b_in, w_mid, b_mid, w_out, border_cols))[:-1]
    prepared = turn_weights(*given)
    own, returned = None, []
    for members in HOME:
        start, home_count = sum(CHUNKS[: members[0]]), sum(CHUNKS[j] for j in members)
        back = []
        for j in members:
            arrived = swap(pieces[4 * j : 4 * j + 4])
            own, back = chemistry(sum(CHUNKS[:j]), (start, home_count), group, prepared, arrived, own, back)
        returned.append(swap(back))
    own, returned[0] = lax.optimization_barrier((own, returned[0]))
    returned = [p for part in returned for p in part]
    owned = lax.all_to_all(own, AXES, 0, 0, axis_index_groups=sides(), tiled=True)
    out = finish(place, middle, border_cols, returned)
    return out.reshape(tracers.shape), deliver(owned)


def solution(mesh):
    return jax.shard_map(
        shards,
        mesh=mesh,
        in_specs=(
            P("spec", None, "tile", None),
            P(None, "tile", None),
            P(None, "tile", None),
            P("tile", None),
            P(),
            P(),
            P(),
            P(),
            P(),
            P(),
        ),
        out_specs=(P("spec", None, "tile", None), P(AXES, None, None)),
        check_vma=False,
    )
```
